256 devices in a mesh: gx: 16 (over y, x), gy: 16 (over z, core).
Axes of the slice: x: 4, y: 4, z: 8, core: 2. Of those that a mesh axis runs over, the one named last changes fastest.
Arguments:
- counts: int32 [2, 16, 256, 4096], P(None, None, 'gx', 'gy'), may hold values from 0 to 8
- classes: int32 [16, 256, 4096], P(None, 'gx', 'gy'), may hold values from 0 to 7
- diffusivity: float32 [2, 8], replicated, may hold values from 0.2 to 5
- cotangent: float32 [2, 16, 256, 4096], P(None, None, 'gx', 'gy'), may hold values from -1203 to 1203
Outputs:
- gradient: float32 [2, 16, 256, 4096], P(None, None, 'gx', 'gy')
The draws below stay inside these ranges and needn't reach their ends.
All inputs are finite; a program needn't handle non-finite values.
Results may differ from the reference program's by a relative error of at most 0.00002.
Values sent between devices are 32-bit elements; how exact they have to be, the bound alone decides.
No kernel may reach another device: no remote copies, remote signals or barrier semaphores. Data moves between devices by JAX's collectives and lax.ppermute only.
A program may use at most 128 MiB of HBM per device.

```python
import math
import jax
import jax.numpy as jnp

NZ = 16
LEVELS = 4
COARSE_SWEEPS = 8
CLASSES = 8
NX = 256
NY = 4096


def smooth_modes(key):
    zpos = jnp.arange(NZ, dtype=jnp.float32)[None, :, None, None]
    xpos = jnp.arange(NX, dtype=jnp.float32)[None, None, :, None]
    ypos = jnp.arange(NY, dtype=jnp.float32)[None, None, None, :]
    total = jnp.zeros((2, NZ, NX, NY), jnp.float32)
    for mode in range(4):
        parts = jax.random.split(jax.random.fold_in(key, mode), 6)
        wave_x = jax.random.uniform(parts[0], (2, 1, 1, 1), jnp.float32, 128.0, 512.0)
        wave_y = jax.random.uniform(parts[1], (2, 1, 1, 1), jnp.float32, 128.0, 512.0)
        sign_y = jnp.where(jax.random.uniform(parts[2], (2, 1, 1, 1)) < 0.5, -1.0, 1.0)
        phase = jax.random.uniform(parts[3], (2, 1, 1, 1), jnp.float32, -math.pi, math.pi)
        amplitude = jax.random.uniform(parts[4], (2, 1, 1, 1), jnp.float32, 0.25, 0.5)
        tilt = jax.random.uniform(parts[5], (2, 1, 1, 1), jnp.float32, 0.0, 1.0)
        angle = 2.0 * math.pi * (xpos / wave_x + sign_y * ypos / wave_y) + phase + math.pi * tilt * zpos / NZ
        total = total + amplitude * jnp.cos(angle)
    return total


def draw_cotangent(key, part):
    key = jax.random.fold_in(key, 7)
    smooth_key, rough_key = jax.random.split(key)
    smooth = smooth_modes(smooth_key)
    rough = 400.0 * jnp.clip(jax.random.normal(rough_key, (2, NZ, NX, NY), jnp.float32), -3.0, 3.0)
    return smooth + rough


def plant(values, rng, smallest, top_value):
    longest = values.shape.index(max(values.shape))
    spots = []
    for shift in (0, 1):
        where = [jax.random.randint(jax.random.fold_in(rng, axis), (), 0, length) for axis, length in enumerate(values.shape)]
        where[longest] = (where[longest] + shift) % values.shape[longest]
        spots.append(tuple(where))
    return values.at[spots[0]].set(smallest).at[spots[1]].set(top_value)


def setup_inputs(seed: int = 0) -> dict:
    key_list = jax.random.split(jax.random.key(seed), 5)
    counts = plant(jax.random.randint(key_list[0], (2, NZ, NX, NY), 0, 9), jax.random.fold_in(key_list[0], 1), 0, 8).astype(jnp.int32)
    classes = plant(jax.random.randint(key_list[1], (NZ, NX, NY), 0, CLASSES), jax.random.fold_in(key_list[1], 1), 0, CLASSES - 1).astype(jnp.int32)
    diffusivity = jnp.clip(jnp.exp(jax.random.uniform(key_list[2], (2, CLASSES), jnp.float32, math.log(0.2), math.log(5.0))), 0.2, 5.0)
    cotangent = draw_cotangent(jax.random.fold_in(key_list[4], 71), 0)
    return {"counts": counts, "classes": classes, "diffusivity": diffusivity, "cotangent": cotangent}


step_time = 256.0
relax = 0.8
react = 0.3


def harmonic(first, second):
    return 2.0 * first * second / (first + second)


def neighbours(padded):
    return (padded[:, 1:-1, :-2, 1:-1], padded[:, 1:-1, 2:, 1:-1],
            padded[:, 1:-1, 1:-1, :-2], padded[:, 1:-1, 1:-1, 2:],
            padded[:, :-2, 1:-1, 1:-1], padded[:, 2:, 1:-1, 1:-1])


def level_weights(dpad, scale):
    centre = dpad[:, 1:-1, 1:-1, 1:-1]
    weights = tuple(harmonic(centre, near) * scale for near in neighbours(dpad))
    total = weights[0]
    for item in weights[1:]:
        total = total + item
    return weights, 1.0 + step_time * total


def apply_operator(upad, weights, diag):
    result = diag * upad[:, 1:-1, 1:-1, 1:-1]
    for weight, near in zip(weights, neighbours(upad)):
        result = result - step_time * weight * near
    return result


def pad_all(field):
    return jnp.pad(field, ((0, 0), (1, 1), (1, 1), (1, 1)))


def coarsen(field):
    shape = field.shape
    return field.reshape(shape[0], shape[1] // 2, 2, shape[2] // 2, 2, shape[3] // 2, 2).mean(axis=(2, 4, 6))


def refine(field):
    return jnp.repeat(jnp.repeat(jnp.repeat(field, 2, axis=1), 2, axis=2), 2, axis=3)


def sweep(field, rhs, weights, diag):
    return field + relax * (rhs - apply_operator(pad_all(field), weights, diag)) / diag


def vcycle(level, rhs, diff):
    weights, diag = level_weights(pad_all(diff), 0.25 ** level)
    field = relax * rhs / diag
    if level == LEVELS:
        for count in range(COARSE_SWEEPS - 1):
            field = sweep(field, rhs, weights, diag)
        resid = rhs - apply_operator(pad_all(field), weights, diag)
        return field + jnp.mean(resid, axis=(1, 2, 3), keepdims=True)
    field = sweep(field, rhs, weights, diag)
    resid = rhs - apply_operator(pad_all(field), weights, diag)
    field = field + refine(vcycle(level + 1, coarsen(resid), coarsen(diff)))
    field = sweep(field, rhs, weights, diag)
    return sweep(field, rhs, weights, diag)


def reference(counts, classes, diffusivity, cotangent):
    diff = jnp.zeros(cotangent.shape, jnp.float32)
    for index in range(CLASSES):
        diff = jnp.where((classes == index)[None], diffusivity[:, index][:, None, None, None], diff)
    adjoint = vcycle(0, cotangent, diff)
    acid = 0.25 * counts[0].astype(jnp.float32)
    quench = 0.25 * counts[1].astype(jnp.float32)
    grad_acid = adjoint[0] * (1.0 - react * quench) - react * quench * adjoint[1]
    grad_quench = adjoint[1] * (1.0 - react * acid) - react * acid * adjoint[0]
    return jnp.stack([grad_acid, grad_quench])
```

```python
import jax
import jax.numpy as jnp
from jax import lax
from jax.experimental import pallas as pl
from jax.experimental.pallas import tpu as pltpu
from jax.sharding import PartitionSpec as P

F32 = jnp.float32
BF16 = jnp.bfloat16
RELAX = 0.8
REACT = 0.3
STEP = 256.0
COARSE_SWEEPS = 8

HX = 4
NPL = 16 + 2 * HX
N1 = 20
HY = 64
LN = 384
PAD = 4
X2 = 64
X3 = 32
X4 = 16


def iota(shape, axis):
    return lax.broadcasted_iota(jnp.int32, shape, axis)


def shift_up(value, by, axis):
    return pltpu.roll(value, by, axis)


def shift_down(value, by, axis):
    return pltpu.roll(value, value.shape[axis] - by, axis)


def reciprocal(x):
    return pl.reciprocal(x, approx=True)


def harm(a, b):
    return a * b * reciprocal(a + b)


def residual(u, b, fx, fxn, wy, wz, sy, sz):
    fy = wy * (u - shift_up(u, sy, 1))
    mu = u + (fx - fxn) + (fy - shift_down(fy, sy, 1))
    fz = wz * (u - shift_up(u, sz, 0))
    return b - (mu + (fz - shift_down(fz, sz, 0)))


def residual_short(u, b, fx, fxn, wy, wz, sy, sz):
    fy = wy * (u - shift_up(u, sy, 1)) - shift_down(wy, sy, 1) * (shift_down(u, sy, 1) - u)
    fz = wz * (u - shift_up(u, sz, 0)) - shift_down(wz, sz, 0) * (shift_down(u, sz, 0) - u)
    return b - (u + (fx - fxn) + (fy + fz))


def diagonal(wx, wxn, wy, wz, sy, sz):
    return 1.0 + (wx + wxn) + (wy + shift_down(wy, sy, 1)) + (wz + shift_down(wz, sz, 0))


def pair_lanes(value, half):
    width = value.shape[1]
    total = value + shift_down(value, half, 1)
    first = (iota(value.shape, 1) // half) % 2 == 0
    return jnp.where(first, total, shift_up(total, half, 1))


def pair_rows(value, half):
    total = value + shift_down(value, half, 0)
    first = (iota(value.shape, 0) // half) % 2 == 0
    return jnp.where(first, total, shift_up(total, half, 0))


def split_store(ref, value):
    for k in range(value.shape[1] // 128):
        ref[k] = value[:, 128 * k : 128 * (k + 1)]


def sum_depth(ref, value):
    rows = value.shape[0]
    split_store(ref, value)
    parts = [
        ref[k, pl.ds(0, rows // 2, stride=2), :] + ref[k, pl.ds(1, rows // 2, stride=2), :]
        for k in range(value.shape[1] // 128)
    ]
    return jnp.concatenate(parts, axis=1)


def spread_depth(ref, value):
    rows = value.shape[0]
    for k in range(3):
        part = value[:, 128 * k : 128 * (k + 1)]
        ref[k, pl.ds(0, rows, stride=2), :] = part
        ref[k, pl.ds(1, rows, stride=2), :] = part
    return jnp.concatenate([ref[k] for k in range(3)], axis=1)


def pick_lanes(value, lanes):
    return jnp.take_along_axis(value, jnp.broadcast_to(lanes, value.shape), axis=1)


def stencil(u, b, wx, wy, wz, start, count, sy, sz):
    here = u[start]
    fx = wx[start] * (here - u[start - 1])
    for j in range(count):
        p = start + j
        after = u[p + 1]
        fxn = wx[p + 1] * (after - here)
        yield p, here, residual(here, b[p], fx, fxn, wy[p], wz[p], sy, sz)
        here, fx = after, fxn


def face_weights(d, wx, wy, wz, inv, b, u, start, count, factor_x, my, mz, sy, sz):
    here = d[start]
    side = factor_x(start) * harm(here, d[start - 1])
    for j in range(count):
        p = start + j
        after = d[p + 1]
        siden = factor_x(p + 1) * harm(after, here)
        y = my * harm(here, shift_up(here, sy, 1))
        z = mz * harm(here, shift_up(here, sz, 0))
        wx[p], wy[p], wz[p] = side, y, z
        value = RELAX * reciprocal(diagonal(side, siden, y, z, sy, sz))
        inv[p] = value
        u[p] = value * b[p]
        here, side = after, siden


def blocks(lo, hi, size, body):
    assert (hi - lo) % size == 0
    if hi - lo == size:
        body(lo)
        return

    def step(n, carry):
        body(lo + n * size)
        return carry

    lax.fori_loop(0, (hi - lo) // size, step, 0)


def table_kernel(diff_ref, table):
    for s in range(2):
        for c in range(8):
            table[pl.ds(8 * s + c, 1), :] = jnp.full((1, 128), diff_ref[s, c], F32)


def turn_kernel(cot, cls, table_in, own, across, inside, table):
    table[...] = table_in[...]
    odd = lax.axis_index("gy") % 2 == 1
    left_half = iota((16, 128), 1) < HY
    for f in range(3):
        for k in range(8):
            pair = []
            for x in (k, k + 8):
                pair.append(cls[:, x, :].astype(F32) if f == 2 else cot[f, :, x, :])
                own[x, f] = pair[-1]
            a, b = pair
            to_left = jnp.where(left_half, a[:, :128], pltpu.roll(b[:, :128], HY, 1))
            to_right = jnp.where(left_half, pltpu.roll(b[:, 128:], HY, 1), a[:, 128:])
            across[k, f] = jnp.where(odd, to_right, to_left)
            inside[k, f] = jnp.where(odd, to_left, to_right)


def cut_strips(planes, first, second):
    odd = lax.axis_index("gx") % 2 == 1
    for f in range(3):
        place = 0 if f == 2 else HX + f * (HX - 1)
        count = HX if f == 2 else HX - 1
        for n in range(count):
            low, high = planes[n, f], planes[16 - count + n, f]
            first[place + n] = jnp.where(odd, high, low)
            second[place + n] = jnp.where(odd, low, high)


def edge_kernel(across, inside, edge, first, second):
    odd = lax.axis_index("gy") % 2 == 1
    left_half = iota((16, 128), 1) < HY
    for k in range(8):
        for f in range(3):
            got = across[k, f], inside[k, f]
            fl, fr = jnp.where(odd, got[1], got[0]), jnp.where(odd, got[0], got[1])
            edge[k, f] = jnp.where(left_half, fr, fl)
            edge[k + 8, f] = pltpu.roll(jnp.where(left_half, fl, fr), HY, 1)
    cut_strips(edge, first, second)


def fine_tools(table, keep0, keep1, d0, v0, d1, zs):
    gx = lax.axis_index("gx")
    gy = lax.axis_index("gy")
    nx = 16 * lax.axis_size("gx")
    ny = 256 * lax.axis_size("gy")
    b0, u0, b1 = keep0.at[0], keep0.at[5], keep1.at[0]

    def look_up(values):
        cls = values.astype(jnp.int32)
        bits = [(cls & (1 << n)) != 0 for n in range(3)]
        out = []
        for s in range(2):
            rows = [jnp.broadcast_to(table[pl.ds(8 * s + c, 1), :], (16, 128)) for c in range(8)]
            rows = [jnp.concatenate([r] * (cls.shape[1] // 128), axis=1) for r in rows]
            rows = [jnp.where(bits[0], rows[2 * n + 1], rows[2 * n]) for n in range(4)]
            rows = [jnp.where(bits[1], rows[2 * n + 1], rows[2 * n]) for n in range(2)]
            out.append(jnp.where(bits[2], rows[1], rows[0]))
        return out

    def assemble_own(own, edge, size):
        def body(start):
            for j in range(size):
                x = start + j
                planes = [jnp.concatenate([own[x, f], edge[x, f]], axis=1) for f in range(3)]
                for s, d in enumerate(look_up(planes[2])):
                    b0[s, x + HX] = planes[s]
                    d0[s, x + HX] = d

        blocks(0, 16, size, body)

    def assemble_strip(main, side, high):
        second = (gx + high) % 2 == 1

        def plane(n):
            return jnp.concatenate(
                [jnp.where(second, b[n], a[n]) for a, b in (main, side)], axis=1
            )

        lo = 20 * high
        for j in range(HX):
            for s, d in enumerate(look_up(plane(j))):
                d0[s, lo + j] = d
        for s in range(2):
            for n in range(HX - 1):
                b0[s, lo + 1 - high + n] = plane(HX + s * (HX - 1) + n)

    def masks(rows, step, factor, origin):
        lane = iota((rows, LN), 1)
        ypos = gy * 256 + jnp.where(lane < 256 + HY, lane, lane - LN)
        my = jnp.where((ypos >= step) & (ypos < ny), F32(factor), F32(0.0))
        mz = jnp.where(iota((rows, LN), 0) >= 1, F32(factor), F32(0.0))

        def factor_x(p):
            xpos = (gx * 16) // step + p - origin
            return jnp.where((xpos >= 1) & (xpos < nx // step), F32(factor), F32(0.0))

        return my, mz, factor_x

    def weigh(lo, hi, size, rows, step, factor, d, keep, v):
        blocks(lo, hi, size, weigher(size, rows, step, factor, d, keep, v))

    def weigher(size, rows, step, factor, d, keep, v):
        my, mz, factor_x = masks(rows, step, factor, HX if step == 1 else 6)

        def body(start):
            for s in range(2):
                face_weights(
                    d.at[s], keep.at[1, s], keep.at[2, s], keep.at[3, s], keep.at[4, s],
                    keep.at[0, s], v.at[s], start, size, factor_x, my, mz, step, 1,
                )

        return body

    def planes(keep, u, s, start, size, step):
        return stencil(
            u.at[s], keep.at[0, s], keep.at[1, s], keep.at[2, s], keep.at[3, s],
            start, size, step, 1,
        )

    def smooth(lo, hi, size, keep, v, step):
        blocks(lo, hi, size, smoother(size, keep, v, step))

    def smoother(size, keep, v, step):
        def body(start):
            for s in range(2):
                for p, here, r in planes(keep, v, s, start, size, step):
                    keep[5, s, p] = here + keep[4, s, p] * r

        return body

    def restrict(lo, hi, size):
        blocks(lo, hi, size, restricter(size))

    def restricter(size):
        def body(start):
            for s in range(2):
                res = [r for _, _, r in planes(keep0, u0, s, 2 * start - 8, 2 * size, 1)]
                for i in range(size):
                    total = pair_lanes(res[2 * i] + res[2 * i + 1], 1)
                    b1[s, start + i] = 0.125 * sum_depth(zs.at[s, i], total)

        return body

    def coarse_diff(lo, hi, size):
        def body(start):
            for i in range(size):
                for s in range(2):
                    p = 2 * (start + i) - 8
                    total = pair_lanes(d0[s, p] + d0[s, p + 1], 1)
                    d1[s, start + i] = 0.125 * sum_depth(zs.at[s, i], total)

        blocks(lo, hi, size, body)

    at = assemble_strip, weigher, smoother, restricter
    return assemble_own, at, weigh, smooth, restrict, coarse_diff, planes


FINE = 2.0 * STEP
COARSER = 0.5 * STEP


def own_kernel(table, own, edge, keep0, keep1, d0, v0, d1, zs):
    assemble_own, _, weigh, smooth, restrict, coarse_diff, _ = fine_tools(
        table, keep0, keep1, d0, v0, d1, zs
    )
    assemble_own(own, edge, 4)
    weigh(5, 19, 7, 16, 1, FINE, d0, keep0, v0)
    smooth(6, 18, 4, keep0, v0, 1)
    restrict(8, 12, 2)
    coarse_diff(6, 14, 4)


def near_kernel(
    table, mfirst, msecond, sfirst, ssecond, keep0_in, keep1_in, d0_in, v0_in, d1_in,
    first, second, keep0, keep1, d0, v0, d1,
    zs,
):
    _, at, _, _, _, _, _ = fine_tools(table, keep0, keep1, d0, v0, d1, zs)
    assemble_strip, weigher, smoother, restricter = at
    weigh = weigher(4, 16, 1, FINE, d0, keep0, v0)
    smooth = smoother(4, keep0, v0, 1)
    restrict = restricter(2)

    def one_side(high, carry):
        assemble_strip((mfirst, msecond), (sfirst, ssecond), high)
        weigh(1 + 18 * high)
        smooth(2 + 16 * high)
        restrict(6 + 6 * high)
        return carry

    lax.fori_loop(0, 2, one_side, 0)
    odd = lax.axis_index("gx") % 2 == 1
    even_lane = iota((8, LN), 1) % 2 == 0

    def send(n, ref, low, high):
        low, high = (jnp.where(even_lane, ref[0, m], ref[1, m]) for m in (low, high))
        first[n] = jnp.where(odd, high, low)
        second[n] = jnp.where(odd, low, high)

    for k in range(4):
        send(k, keep1.at[0], 6 + k, 10 + k)
    for k in range(5):
        send(4 + k, d1, 6 + k, 9 + k)


def averaging(shape, dtype):
    group = iota(shape, 0) // 4
    target = jnp.where(group < (256 + HY) // 4, group + 16, group - 80)
    return jnp.where(iota(shape, 1) == target, F32(0.0625), F32(0.0)).astype(dtype)


def to_level2(rows, matrix, zs, message):
    rows = jnp.concatenate(rows, axis=0)
    high = rows.astype(BF16)
    rest = rows - high.astype(F32)
    middle = rest.astype(BF16)
    low = (rest - middle.astype(F32)).astype(BF16)
    whole = jnp.dot(
        jnp.concatenate([high, middle, low], axis=0), matrix, preferred_element_type=F32
    )
    whole = whole[0:64] + whole[64:128] + whole[128:192]
    lane = iota((8, 128), 1)
    halved = []
    for n in range(4):
        part = zs.at[0, n, 0]
        part[...] = whole[16 * n : 16 * (n + 1)]
        halved.append(part[pl.ds(0, 8, stride=2), :] + part[pl.ds(1, 8, stride=2), :])
    for k in range(3):
        message[k] = jnp.where(lane < 96, halved[k], pltpu.roll(halved[3], 96 - 32 * k, 1))


def inner_kernel(keep1_in, d1, counts, keep1, v1, react, diff2, matrix, zs):
    _, _, weigh, smooth, _, _, _ = fine_tools(None, keep1, keep1, None, None, d1, zs)
    weigh(7, 13, 6, 8, 2, COARSER, d1, keep1, v1)
    smooth(8, 12, 4, keep1, v1, 2)
    for s in range(2):
        for x in range(16):
            react[x, s] = REACT * (0.25 * counts[s, :, x, :].astype(F32))
    matrix[...] = averaging((LN, 128), BF16)
    rows = [d1[s, 6 + 2 * n] + d1[s, 7 + 2 * n] for n in range(4) for s in range(2)]
    to_level2(rows, matrix[...], zs, diff2)


def outer_kernel(
    first, second, diff2, matrix, keep1_in, v1_in, d1_in,
    message, keep1, v1, d1,
    zs,
):
    _, _, weigh, smooth, _, _, planes = fine_tools(None, keep1, keep1, None, None, d1, zs)
    gx = lax.axis_index("gx")
    last = lax.axis_size("gx") - 1
    odd = gx % 2 == 1
    even_lane = iota((8, LN), 1) % 2 == 0

    def both(got, ref, m, real=None):
        if real is not None:
            got = jnp.where(real, got, F32(1.0))
        ref[0, m] = jnp.where(even_lane, got, shift_up(got, 1, 1))
        ref[1, m] = jnp.where(even_lane, shift_down(got, 1, 1), got)

    for k in range(9):
        low = jnp.where(odd, second[k], first[k])
        high = jnp.where(odd, first[k], second[k])
        if k < 4:
            both(low, keep1.at[0], 2 + k)
            both(high, keep1.at[0], 14 + k)
        else:
            both(low, d1, k - 3, gx > 0)
            both(high, d1, 10 + k, gx < last)
    for start in (2, 13):
        weigh(start, start + 5, 5, 8, 2, COARSER, d1, keep1, v1)
    for start in (3, 12):
        smooth(start, start + 5, 5, keep1, v1, 2)
    res = [[r for _, _, r in planes(keep1, keep1.at[5], s, 6, 8, 2)] for s in range(2)]
    rows = [res[s][2 * n] + res[s][2 * n + 1] for n in range(4) for s in range(2)]
    to_level2(rows, matrix[...], zs, message.at[0])
    message[1] = diff2[...]


def middle_kernel(gathered, tile, keep2, keep3, d2, d3, v2, v3, coarse):
    gy = lax.axis_index("gy")
    ny = 256 * lax.axis_size("gy")
    lane = iota((8, 128), 1)
    row = iota((8, 128), 0)
    ypos = gy * 64 + lane - 16
    zero = jnp.zeros((8, 128), F32)

    for keep, d, v, count in ((keep2, d2, v2, X2), (keep3, d3, v3, X3)):
        for k in range(PAD):
            for n in range(6):
                keep[n, k] = zero
                keep[n, count + PAD + k] = zero
        for p in (PAD - 1, PAD + count):
            d[p] = zero + 1.0
            v[p] = zero

    def level(keep, d, v, count, size, sy, sz, scale, nyl):
        factor = 2.0 * STEP * scale
        my = jnp.where((ypos >= sy) & (ypos < nyl), F32(factor), F32(0.0))
        mz = jnp.where(row % 4 >= sz, F32(factor), F32(0.0))

        def factor_x(p):
            return jnp.where((p > PAD) & (p < PAD + count), F32(factor), F32(0.0))

        def weights(start):
            face_weights(
                d, keep.at[1], keep.at[2], keep.at[3], keep.at[4], keep.at[0], v,
                start, size, factor_x, my, mz, sy, sz,
            )

        def planes(u, start, amount):
            return stencil(
                u, keep.at[0], keep.at[1], keep.at[2], keep.at[3], start, amount, sy, sz
            )

        def smooth(start):
            for p, here, r in planes(v, start, count):
                keep[5, p] = here + keep[4, p] * r

        blocks(PAD, PAD + count, size, weights)
        blocks(PAD, PAD + count, count, smooth)
        return planes

    for g in range(X2 // 4):
        for f, ref in ((0, keep2.at[0]), (1, d2)):
            packed = [gathered[g, f, k] for k in range(3)]
            fourth = [pltpu.roll(packed[k], 32 * (k + 1), 1) for k in range(3)]
            fourth = jnp.where(lane < 32, fourth[0], jnp.where(lane < 64, fourth[1], fourth[2]))
            for k, plane in enumerate(packed + [fourth]):
                ref[PAD + 4 * g + k] = plane
    planes2 = level(keep2, d2, v2, X2, 32, 1, 1, 0.0625, ny // 4)

    def restrict(start):
        first = 2 * (start - PAD) + PAD
        res = [r for _, _, r in planes2(keep2.at[5], first, 32)]
        for i in range(16):
            total = res[2 * i] + res[2 * i + 1]
            keep3[0, start + i] = 0.125 * pair_rows(pair_lanes(total, 1), 1)
            total = d2[first + 2 * i] + d2[first + 2 * i + 1]
            d3[start + i] = 0.125 * pair_rows(pair_lanes(total, 1), 1)

    blocks(PAD, PAD + X3, 16, restrict)
    planes3 = level(keep3, d3, v3, X3, 32, 2, 2, 0.015625, ny // 4)

    def gather_pair(total):
        total = total + shift_down(total, 2, 1)
        return total + shift_down(total, 2, 0)

    res = [r for _, _, r in planes3(keep3.at[5], PAD, X3)]
    for i in range(X4):
        coarse[0, pl.ds(8 * i, 8), :] = gather_pair(res[2 * i] + res[2 * i + 1])
        coarse[1, pl.ds(8 * i, 8), :] = gather_pair(d3[PAD + 2 * i] + d3[PAD + 2 * i + 1])
    total = jnp.zeros((8, 128), F32)
    for g in range(8):
        f, s, half = g // 4, (g // 2) % 2, g % 2
        part = coarse[f, pl.ds(64 * half + 4 * s, 8, stride=8), :]
        part = pick_lanes(part, 16 + 4 * (lane % 16))
        total = jnp.where(lane // 16 == g, part, total)
    tile[...] = 0.125 * total


def coarsest(tiles):
    ngy = tiles.shape[0]
    width = 16 * ngy
    lane_group = iota((8, 128), 1) // 16
    fields = []
    for g in range(8):
        halves = []
        for h in range(width // 128):
            total = jnp.zeros((8, 128), F32)
            for q in range(8):
                piece = tiles[8 * h + q]
                shift = (16 * q - 16 * g) % 128
                if shift:
                    piece = pltpu.roll(piece, shift, 1)
                total = jnp.where(lane_group == q, piece, total)
            halves.append(total)
        fields.append(jnp.concatenate(halves, axis=1))
    whole = [jnp.concatenate([fields[2 * n], fields[2 * n + 1]], axis=0) for n in range(4)]
    shape = whole[0].shape
    factor = 2.0 * STEP * 0.25**4
    mx = jnp.where(iota(shape, 0) >= 1, F32(factor), F32(0.0))
    my = jnp.where(iota(shape, 1) >= 1, F32(factor), F32(0.0))
    out = []
    for s in range(2):
        b, d = whole[s], whole[2 + s]
        wx = mx * harm(d, shift_up(d, 1, 0))
        wy = my * harm(d, shift_up(d, 1, 1))
        inv = RELAX / (1.0 + (wx + shift_down(wx, 1, 0)) + (wy + shift_down(wy, 1, 1)))

        u = start = inv * b
        up_x, down_x = inv * wx, inv * shift_down(wx, 1, 0)
        up_y, down_y = inv * wy, inv * shift_down(wy, 1, 1)
        for _ in range(COARSE_SWEEPS - 1):
            along_x = up_x * shift_up(u, 1, 0) + down_x * shift_down(u, 1, 0)
            along_y = up_y * shift_up(u, 1, 1) + down_y * shift_down(u, 1, 1)
            u = ((1.0 - RELAX) * u + start) + (along_x + along_y)
        out.append(u + jnp.sum(b - u) / (shape[0] * shape[1]))
    return out


def up_kernel(
    tiles, keep2, keep3, keep0, keep1, react,
    out,
    c4, rep2, u3, u2, c2, p1, q1, q0, zs,
):
    gx = lax.axis_index("gx")
    gy = lax.axis_index("gy")

    solved = jnp.concatenate(coarsest(tiles), axis=0)
    width = solved.shape[1]
    solved = pltpu.roll(solved, (width + 4 - 16 * gy) % width, 1)[:, :128]
    near = pick_lanes(solved, iota((1, 128), 1) // 4)
    for t in range(2):
        c4[t, pl.ds(0, 8), :] = jnp.zeros((8, 128), F32)
        c4[t, pl.ds(8, X4), :] = near[X4 * t : X4 * (t + 1)]
        c4[t, pl.ds(8 + X4, 8), :] = jnp.zeros((8, 128), F32)
    first_species = iota((8, 128), 0) < 4

    def coarse_plane(k):
        rows = [
            jnp.broadcast_to(c4[t, pl.ds(gx + 6 + k, 1), :], (8, 128)) for t in range(2)
        ]
        return jnp.where(first_species, rows[0], rows[1])

    def sweeps(keep, base, u, count, sy, sz):
        for turn in range(2):
            lo, hi = 1 + turn, count - 1 - turn
            here = u[lo]
            fx = keep[1, base + lo] * (here - u[lo - 1])
            for i in range(lo, hi):
                after = u[i + 1]
                fxn = keep[1, base + i + 1] * (after - here)
                r = residual_short(
                    here, keep[0, base + i], fx, fxn,
                    keep[2, base + i], keep[3, base + i], sy, sz,
                )
                u[i] = here + keep[4, base + i] * r
                here, fx = after, fxn

    base3 = gx * 2
    for i in range(0, 10, 2):
        plane = coarse_plane(i // 2)
        u3[i] = keep3[5, base3 + i] + plane
        u3[i + 1] = keep3[5, base3 + i + 1] + plane
    sweeps(keep3, base3, u3, 10, 2, 2)
    base2 = gx * 4
    for i in range(12):
        u2[i] = keep2[5, base2 + i] + u3[min(2 + i // 2, 9)]
    sweeps(keep2, base2, u2, 12, 1, 1)

    for i in range(8):
        for k in range(2):
            rep2[pl.ds(16 * i + k, 8, stride=2), :] = u2[2 + i]
    quarter = iota((1, 128), 1) // 4
    edge = jnp.where(quarter < 16, quarter + 80, quarter - 16)
    flat = [pick_lanes(rep2[...], lanes) for lanes in (quarter + 16, quarter + 48, edge)]
    flat = jnp.concatenate(flat, axis=1)
    c2[...] = flat.reshape(8, 2, 8, LN)

    def planes(keep, u, s, start, size, step):
        return stencil(
            u.at[s], keep.at[0, s], keep.at[1, s], keep.at[2, s], keep.at[3, s],
            start, size, step, 1,
        )

    def smooth(lo, hi, size, keep, u, new, step):
        def body(start):
            for s in range(2):
                for p, here, r in planes(keep, u, s, start, size, step):
                    new[s, p] = here + keep[4, s, p] * r

        blocks(lo, hi, size, body)

    for i in range(3, 17):
        for s in range(2):
            p1[s, i] = keep1[5, s, i] + c2[(i - 6) // 2 + 2, s]
    smooth(4, 16, 12, keep1, p1, q1, 2)
    smooth(5, 15, 10, keep1, q1, p1, 2)

    def corrected_sweep(n, carry):
        start = 3 + 6 * n
        for s in range(2):
            spread = [spread_depth(zs.at[s, j], p1[s, 5 + 3 * n + j]) for j in range(4)]
            u = [keep0[5, s, start - 1 + j] + spread[j // 2] for j in range(8)]
            fx = keep0[1, s, start] * (u[1] - u[0])
            for j in range(6):
                p = start + j
                fxn = keep0[1, s, p + 1] * (u[j + 2] - u[j + 1])
                r = residual(
                    u[j + 1], keep0[0, s, p], fx, fxn, keep0[2, s, p], keep0[3, s, p], 1, 1
                )
                q0[s, p] = u[j + 1] + keep0[4, s, p] * r
                fx = fxn
        return carry

    lax.fori_loop(0, 3, corrected_sweep, 0)

    def last(start):
        adj = [[], []]
        for s in range(2):
            for p, here, r in planes(keep0, q0, s, start, 4, 1):
                adj[s].append((here + keep0[4, s, p] * r)[:, :256])
        for j in range(4):
            x = start + j - HX
            a0, a1 = adj[0][j], adj[1][j]
            total = a0 + a1
            out[0, :, x, :] = a0 - react[x, 1] * total
            out[1, :, x, :] = a1 - react[x, 0] * total

    blocks(4, 20, 4, last)


def call(
    kernel, outs, scratch, args, name, limit, kinds=None, aliases=None, cycles=0, dtypes=None
):
    spaces = {"v": pltpu.VMEM, "s": pltpu.SMEM}
    specs = [pl.BlockSpec(memory_space=spaces[k]) for k in kinds or "v" * len(args)]
    return pl.pallas_call(
        kernel,
        out_shape=[jax.ShapeDtypeStruct(o, d) for o, d in zip(outs, dtypes or [F32] * len(outs))],
        in_specs=specs,
        out_specs=[pl.BlockSpec(memory_space=pltpu.VMEM)] * len(outs),
        scratch_shapes=[pltpu.VMEM(s, F32) if isinstance(s, tuple) else s for s in scratch],
        input_output_aliases=aliases or {},
        compiler_params=pltpu.CompilerParams(vmem_limit_bytes=limit * 1024 * 1024),
        cost_estimate=pl.CostEstimate(flops=cycles, bytes_accessed=0, transcendentals=0)
        if cycles
        else None,
        name=name,
    )(*args)


def swap(axis, first, block):
    pairs = [(i, i + 1) for i in range(first, lax.axis_size(axis) - 1, 2)]
    return lax.ppermute(block, axis, pairs + [(j, i) for i, j in pairs])


def everyone(block, axis):
    count = lax.axis_size(axis)
    copies = jnp.broadcast_to(block[None], (count,) + block.shape)
    return lax.all_to_all(copies, axis, split_axis=0, concat_axis=0, tiled=True)


def per_device(counts, classes, diffusivity, cotangent):
    (table,) = call(table_kernel, [(16, 128)], [], (diffusivity,), "table", 8, "s", cycles=10**9)
    own, across, inside, table = call(
        turn_kernel,
        [(16, 3, 16, 256), (8, 3, 16, 128), (8, 3, 16, 128), (16, 128)], [],
        (cotangent, classes, table), "turn", 8,
    )
    across, inside = swap("gy", 1, across), swap("gy", 0, inside)
    strip = (3 * HX - 2, 16, 256)
    mfirst, msecond = call(cut_strips, [strip, strip], [], (own,), "strips", 8)
    mfirst, msecond = swap("gx", 1, mfirst), swap("gx", 0, msecond)
    strip = (3 * HX - 2, 16, 128)
    edge, sfirst, ssecond = call(
        edge_kernel, [(16, 3, 16, 128), strip, strip], [], (across, inside), "edge", 8
    )
    sfirst, ssecond = swap("gx", 1, sfirst), swap("gx", 0, ssecond)
    fine = [(6, 2, NPL, 16, LN), (6, 2, N1, 8, LN)]
    fine += [(2, NPL, 16, LN)] * 2 + [(2, N1, 8, LN)]
    zs = (2, 4, 3, 16, 128)
    kept = call(own_kernel, fine, [zs], (table, own, edge), "own", 8, cycles=10**7)
    strip = (9, 8, LN)
    first, second, keep0, keep1, _, _, d1 = call(
        near_kernel,
        [strip, strip] + fine, [zs],
        (table, mfirst, msecond, sfirst, ssecond, *kept), "near", 8,
        aliases={5 + n: 2 + n for n in range(5)},
    )
    first, second = swap("gx", 1, first), swap("gx", 0, second)
    level1 = [(6, 2, N1, 8, LN), (2, N1, 8, LN), (2, N1, 8, LN)]
    zs = (2, 5, 3, 16, 128)
    keep1, v1, react, diff2, matrix = call(
        inner_kernel, level1[:2] + [(16, 2, 16, 256), (3, 8, 128), (LN, 128)], [zs],
        (keep1, d1, counts), "inner", 8,
        aliases={0: 0}, cycles=10**7, dtypes=[F32] * 4 + [BF16],
    )
    message, keep1, _, _ = call(
        outer_kernel, [(2, 3, 8, 128)] + level1, [zs],
        (first, second, diff2, matrix, keep1, v1, d1), "outer", 8,
        aliases={4: 1, 5: 2, 6: 3},
    )
    gathered = everyone(message, "gx")
    tile, keep2, keep3 = call(
        middle_kernel,
        [(8, 128), (6, X2 + 2 * PAD, 8, 128), (6, X3 + 2 * PAD, 8, 128)],
        [(X2 + 2 * PAD, 8, 128), (X3 + 2 * PAD, 8, 128)] * 2 + [(2, 128, 128)],
        (gathered,), "middle", 8,
    )
    tiles = everyone(tile, "gy")
    (gradient,) = call(
        up_kernel,
        [(2, 16, 16, 256)],
        [
            (2, X4 + 16, 128), (128, 128), (10, 8, 128), (12, 8, 128), (8, 2, 8, LN),
            (2, N1, 8, LN), (2, N1, 8, LN), (2, NPL, 16, LN),
            (2, 5, 3, 16, 128),
        ],
        (tiles, keep2, keep3, keep0, keep1, react), "up", 12,
    )
    return gradient


def solution(mesh):
    in_specs = (P(None, None, "gx", "gy"), P(None, "gx", "gy"), P(), P(None, None, "gx", "gy"))
    out_specs = P(None, None, "gx", "gy")
    return jax.shard_map(
        per_device, mesh=mesh, in_specs=in_specs, out_specs=out_specs, check_vma=False
    )
```

```python
import jax
import jax.numpy as jnp
from jax import lax
from jax.experimental import pallas as pl
from jax.experimental.pallas import tpu as pltpu
from jax.sharding import PartitionSpec as P

F32 = jnp.float32
BF16 = jnp.bfloat16
RELAX = 0.8
REACT = 0.3
STEP = 256.0
COARSE_SWEEPS = 8

HX = 4
NPL = 16 + 2 * HX
N1 = 20
HY = 64
LN = 384
PAD = 4
X2 = 64
X3 = 32
X4 = 16


def iota(shape, axis):
    return lax.broadcasted_iota(jnp.int32, shape, axis)


def shift_up(value, by, axis):
    return pltpu.roll(value, by, axis)


def shift_down(value, by, axis):
    return pltpu.roll(value, value.shape[axis] - by, axis)


def reciprocal(x):
    return pl.reciprocal(x, approx=True)


def z_up(value, step):
    if step:
        return shift_up(value, step, 0)
    return jnp.concatenate([shift_up(value[8:], 1, 0), value[:8]], axis=0)


def z_down(value, step):
    if step:
        return shift_down(value, step, 0)
    return jnp.concatenate([value[8:], shift_down(value[:8], 1, 0)], axis=0)


def harm(a, b):
    return a * b * reciprocal(a + b)


def residual(u, b, fx, fxn, wy, wz, sy, sz):
    fy = wy * (u - shift_up(u, sy, 1))
    mu = u + (fx - fxn) + (fy - shift_down(fy, sy, 1))
    fz = wz * (u - z_up(u, sz))
    return b - (mu + (fz - z_down(fz, sz)))


def residual_short(u, b, fx, fxn, wy, wz, sy, sz):
    fy = wy * (u - shift_up(u, sy, 1)) - shift_down(wy, sy, 1) * (shift_down(u, sy, 1) - u)
    fz = wz * (u - z_up(u, sz)) - z_down(wz, sz) * (z_down(u, sz) - u)
    return b - (u + (fx - fxn) + (fy + fz))


def diagonal(wx, wxn, wy, wz, sy, sz):
    return 1.0 + (wx + wxn) + (wy + shift_down(wy, sy, 1)) + (wz + z_down(wz, sz))


def pair_lanes(value, half):
    width = value.shape[1]
    total = value + shift_down(value, half, 1)
    first = (iota(value.shape, 1) // half) % 2 == 0
    return jnp.where(first, total, shift_up(total, half, 1))


def pair_rows(value, half):
    total = value + shift_down(value, half, 0)
    first = (iota(value.shape, 0) // half) % 2 == 0
    return jnp.where(first, total, shift_up(total, half, 0))


def pick_lanes(value, lanes):
    return jnp.take_along_axis(value, jnp.broadcast_to(lanes, value.shape), axis=1)


def stencil(u, b, wx, wy, wz, start, count, sy, sz):
    here = u[start]
    fx = wx[start] * (here - u[start - 1])
    for j in range(count):
        p = start + j
        after = u[p + 1]
        fxn = wx[p + 1] * (after - here)
        yield p, here, residual(here, b[p], fx, fxn, wy[p], wz[p], sy, sz)
        here, fx = after, fxn


def face_weights(d, wx, wy, wz, inv, b, u, start, count, factor_x, my, mz, sy, sz):
    here = d[start]
    side = factor_x(start) * harm(here, d[start - 1])
    for j in range(count):
        p = start + j
        after = d[p + 1]
        siden = factor_x(p + 1) * harm(after, here)
        y = my * harm(here, shift_up(here, sy, 1))
        z = mz * harm(here, z_up(here, sz))
        wx[p], wy[p], wz[p] = side, y, z
        value = RELAX * reciprocal(diagonal(side, siden, y, z, sy, sz))
        inv[p] = value
        u[p] = value * b[p]
        here, side = after, siden


def blocks(lo, hi, size, body):
    assert (hi - lo) % size == 0
    if hi - lo == size:
        body(lo)
        return

    def step(n, carry):
        body(lo + n * size)
        return carry

    lax.fori_loop(0, (hi - lo) // size, step, 0)


def table_kernel(diff_ref, table):
    for s in range(2):
        for c in range(8):
            table[pl.ds(8 * s + c, 1), :] = jnp.full((1, 128), diff_ref[s, c], F32)


def turn_kernel(cot, cls, table_in, own, across, inside, table):
    table[...] = table_in[...]
    odd = lax.axis_index("gy") % 2 == 1
    left_half = iota((16, 128), 1) < HY
    for f in range(3):
        for k in range(8):
            pair = []
            for x in (k, k + 8):
                halves = [cls[:, n, x, :] if f == 2 else cot[f, :, n, x, :] for n in range(2)]
                pair.append(jnp.concatenate(halves, axis=0).astype(F32))
                own[x, f] = pair[-1]
            a, b = pair
            to_left = jnp.where(left_half, a[:, :128], pltpu.roll(b[:, :128], HY, 1))
            to_right = jnp.where(left_half, pltpu.roll(b[:, 128:], HY, 1), a[:, 128:])
            across[k, f] = jnp.where(odd, to_right, to_left)
            inside[k, f] = jnp.where(odd, to_left, to_right)


def cut_strips(planes, first, second):
    odd = lax.axis_index("gx") % 2 == 1
    for f in range(3):
        place = 0 if f == 2 else HX + f * (HX - 1)
        count = HX if f == 2 else HX - 1
        for n in range(count):
            low, high = planes[n, f], planes[16 - count + n, f]
            first[place + n] = jnp.where(odd, high, low)
            second[place + n] = jnp.where(odd, low, high)


def edge_kernel(across, inside, edge, first, second):
    odd = lax.axis_index("gy") % 2 == 1
    left_half = iota((16, 128), 1) < HY
    for k in range(8):
        for f in range(3):
            got = across[k, f], inside[k, f]
            fl, fr = jnp.where(odd, got[1], got[0]), jnp.where(odd, got[0], got[1])
            edge[k, f] = jnp.where(left_half, fr, fl)
            edge[k + 8, f] = pltpu.roll(jnp.where(left_half, fl, fr), HY, 1)
    cut_strips(edge, first, second)


def fine_tools(table, keep0, keep1, d0, v0, d1):
    gx = lax.axis_index("gx")
    gy = lax.axis_index("gy")
    nx = 16 * lax.axis_size("gx")
    ny = 256 * lax.axis_size("gy")
    b0, u0, b1 = keep0.at[0], keep0.at[5], keep1.at[0]

    def look_up(values):
        cls = values.astype(jnp.int32)
        bits = [(cls & (1 << n)) != 0 for n in range(3)]
        out = []
        for s in range(2):
            rows = [jnp.broadcast_to(table[pl.ds(8 * s + c, 1), :], (16, 128)) for c in range(8)]
            rows = [jnp.concatenate([r] * (cls.shape[1] // 128), axis=1) for r in rows]
            rows = [jnp.where(bits[0], rows[2 * n + 1], rows[2 * n]) for n in range(4)]
            rows = [jnp.where(bits[1], rows[2 * n + 1], rows[2 * n]) for n in range(2)]
            out.append(jnp.where(bits[2], rows[1], rows[0]))
        return out

    def assemble_own(own, edge, size):
        def body(start):
            for j in range(size):
                x = start + j
                planes = [jnp.concatenate([own[x, f], edge[x, f]], axis=1) for f in range(3)]
                for s, d in enumerate(look_up(planes[2])):
                    b0[s, x + HX] = planes[s]
                    d0[s, x + HX] = d

        blocks(0, 16, size, body)

    def assemble_strip(main, side, high):
        second = (gx + high) % 2 == 1

        def plane(n):
            return jnp.concatenate(
                [jnp.where(second, b[n], a[n]) for a, b in (main, side)], axis=1
            )

        lo = 20 * high
        for j in range(HX):
            for s, d in enumerate(look_up(plane(j))):
                d0[s, lo + j] = d
        for s in range(2):
            for n in range(HX - 1):
                b0[s, lo + 1 - high + n] = plane(HX + s * (HX - 1) + n)

    def masks(rows, step, factor, origin):
        lane = iota((rows, LN), 1)
        ypos = gy * 256 + jnp.where(lane < 256 + HY, lane, lane - LN)
        my = jnp.where((ypos >= step) & (ypos < ny), F32(factor), F32(0.0))
        mz = jnp.where(iota((rows, LN), 0) >= 1, F32(factor), F32(0.0))

        def factor_x(p):
            xpos = (gx * 16) // step + p - origin
            return jnp.where((xpos >= 1) & (xpos < nx // step), F32(factor), F32(0.0))

        return my, mz, factor_x

    def weigh(lo, hi, size, rows, step, factor, d, keep, v):
        blocks(lo, hi, size, weigher(size, rows, step, factor, d, keep, v))

    def weigher(size, rows, step, factor, d, keep, v):
        my, mz, factor_x = masks(rows, step, factor, HX if step == 1 else 6)

        def body(start):
            for s in range(2):
                face_weights(
                    d.at[s], keep.at[1, s], keep.at[2, s], keep.at[3, s], keep.at[4, s],
                    keep.at[0, s], v.at[s], start, size, factor_x, my, mz, step, 0 if step == 1 else 1,
                )

        return body

    def planes(keep, u, s, start, size, step):
        return stencil(
            u.at[s], keep.at[0, s], keep.at[1, s], keep.at[2, s], keep.at[3, s],
            start, size, step, 0 if step == 1 else 1,
        )

    def smooth(lo, hi, size, keep, v, step):
        blocks(lo, hi, size, smoother(size, keep, v, step))

    def smoother(size, keep, v, step):
        def body(start):
            for s in range(2):
                for p, here, r in planes(keep, v, s, start, size, step):
                    keep[5, s, p] = here + keep[4, s, p] * r

        return body

    def restrict(lo, hi, size):
        blocks(lo, hi, size, restricter(size))

    def restricter(size):
        def body(start):
            for s in range(2):
                res = [r for _, _, r in planes(keep0, u0, s, 2 * start - 8, 2 * size, 1)]
                for i in range(size):
                    total = res[2 * i] + res[2 * i + 1]
                    b1[s, start + i] = 0.125 * pair_lanes(total[:8] + total[8:], 1)

        return body

    def coarse_diff(lo, hi, size):
        def body(start):
            for i in range(size):
                for s in range(2):
                    p = 2 * (start + i) - 8
                    total = d0[s, p] + d0[s, p + 1]
                    d1[s, start + i] = 0.125 * pair_lanes(total[:8] + total[8:], 1)

        blocks(lo, hi, size, body)

    at = assemble_strip, weigher, smoother, restricter
    return assemble_own, at, weigh, smooth, restrict, coarse_diff, planes


FINE = 2.0 * STEP
COARSER = 0.5 * STEP


def own_kernel(table, own, edge, keep0, keep1, d0, v0, d1):
    assemble_own, _, weigh, smooth, restrict, coarse_diff, _ = fine_tools(
        table, keep0, keep1, d0, v0, d1
    )
    assemble_own(own, edge, 4)
    weigh(5, 19, 7, 16, 1, FINE, d0, keep0, v0)
    smooth(6, 18, 4, keep0, v0, 1)
    restrict(8, 12, 2)
    coarse_diff(6, 14, 4)


def near_kernel(
    table, mfirst, msecond, sfirst, ssecond, keep0_in, keep1_in, d0_in, v0_in, d1_in,
    first, second, keep0, keep1, d0, v0, d1,
):
    _, at, _, _, _, _, _ = fine_tools(table, keep0, keep1, d0, v0, d1)
    assemble_strip, weigher, smoother, restricter = at
    weigh = weigher(4, 16, 1, FINE, d0, keep0, v0)
    smooth = smoother(4, keep0, v0, 1)
    restrict = restricter(2)

    def one_side(high, carry):
        assemble_strip((mfirst, msecond), (sfirst, ssecond), high)
        weigh(1 + 18 * high)
        smooth(2 + 16 * high)
        restrict(6 + 6 * high)
        return carry

    lax.fori_loop(0, 2, one_side, 0)
    odd = lax.axis_index("gx") % 2 == 1
    even_lane = iota((8, LN), 1) % 2 == 0

    def send(n, ref, low, high):
        low, high = (jnp.where(even_lane, ref[0, m], ref[1, m]) for m in (low, high))
        first[n] = jnp.where(odd, high, low)
        second[n] = jnp.where(odd, low, high)

    for k in range(4):
        send(k, keep1.at[0], 6 + k, 10 + k)
    for k in range(5):
        send(4 + k, d1, 6 + k, 9 + k)


def averaging(shape, dtype):
    group = iota(shape, 0) // 4
    target = jnp.where(group < (256 + HY) // 4, group + 16, group - 80)
    return jnp.where(iota(shape, 1) == target, F32(0.0625), F32(0.0)).astype(dtype)


def to_level2(rows, matrix, zs, message):
    rows = jnp.concatenate(rows, axis=0)
    high = rows.astype(BF16)
    rest = rows - high.astype(F32)
    middle = rest.astype(BF16)
    low = (rest - middle.astype(F32)).astype(BF16)
    whole = jnp.dot(
        jnp.concatenate([high, middle, low], axis=0), matrix, preferred_element_type=F32
    )
    whole = whole[0:64] + whole[64:128] + whole[128:192]
    lane = iota((8, 128), 1)
    halved = []
    for n in range(4):
        part = zs.at[n]
        part[...] = whole[16 * n : 16 * (n + 1)]
        halved.append(part[pl.ds(0, 8, stride=2), :] + part[pl.ds(1, 8, stride=2), :])
    for k in range(3):
        message[k] = jnp.where(lane < 96, halved[k], pltpu.roll(halved[3], 96 - 32 * k, 1))


def inner_kernel(keep1_in, d1, counts, keep1, v1, react, diff2, matrix, zs):
    _, _, weigh, smooth, _, _, _ = fine_tools(None, keep1, keep1, None, None, d1)
    weigh(7, 13, 6, 8, 2, COARSER, d1, keep1, v1)
    smooth(8, 12, 4, keep1, v1, 2)
    for s in range(2):
        for x in range(16):
            halves = [counts[s, :, n, x, :] for n in range(2)]
            react[x, s] = REACT * (0.25 * jnp.concatenate(halves, axis=0).astype(F32))
    matrix[...] = averaging((LN, 128), BF16)
    rows = [d1[s, 6 + 2 * n] + d1[s, 7 + 2 * n] for n in range(4) for s in range(2)]
    to_level2(rows, matrix[...], zs, diff2)


def outer_kernel(
    first, second, diff2, matrix, keep1_in, v1_in, d1_in,
    message, keep1, v1, d1,
    zs,
):
    _, _, weigh, smooth, _, _, planes = fine_tools(None, keep1, keep1, None, None, d1)
    gx = lax.axis_index("gx")
    last = lax.axis_size("gx") - 1
    odd = gx % 2 == 1
    even_lane = iota((8, LN), 1) % 2 == 0

    def both(got, ref, m, real=None):
        if real is not None:
            got = jnp.where(real, got, F32(1.0))
        ref[0, m] = jnp.where(even_lane, got, shift_up(got, 1, 1))
        ref[1, m] = jnp.where(even_lane, shift_down(got, 1, 1), got)

    for k in range(9):
        low = jnp.where(odd, second[k], first[k])
        high = jnp.where(odd, first[k], second[k])
        if k < 4:
            both(low, keep1.at[0], 2 + k)
            both(high, keep1.at[0], 14 + k)
        else:
            both(low, d1, k - 3, gx > 0)
            both(high, d1, 10 + k, gx < last)
    for start in (2, 13):
        weigh(start, start + 5, 5, 8, 2, COARSER, d1, keep1, v1)
    for start in (3, 12):
        smooth(start, start + 5, 5, keep1, v1, 2)
    res = [[r for _, _, r in planes(keep1, keep1.at[5], s, 6, 8, 2)] for s in range(2)]
    rows = [res[s][2 * n] + res[s][2 * n + 1] for n in range(4) for s in range(2)]
    to_level2(rows, matrix[...], zs, message.at[0])
    message[1] = diff2[...]


def middle_kernel(gathered, tile, keep2, keep3, d2, d3, v2, v3, coarse):
    gy = lax.axis_index("gy")
    ny = 256 * lax.axis_size("gy")
    lane = iota((8, 128), 1)
    row = iota((8, 128), 0)
    ypos = gy * 64 + lane - 16
    zero = jnp.zeros((8, 128), F32)

    for keep, d, v, count in ((keep2, d2, v2, X2), (keep3, d3, v3, X3)):
        for k in range(PAD):
            for n in range(6):
                keep[n, k] = zero
                keep[n, count + PAD + k] = zero
        for p in (PAD - 1, PAD + count):
            d[p] = zero + 1.0
            v[p] = zero

    def level(keep, d, v, count, size, sy, sz, scale, nyl):
        factor = 2.0 * STEP * scale
        my = jnp.where((ypos >= sy) & (ypos < nyl), F32(factor), F32(0.0))
        mz = jnp.where(row % 4 >= sz, F32(factor), F32(0.0))

        def factor_x(p):
            return jnp.where((p > PAD) & (p < PAD + count), F32(factor), F32(0.0))

        def weights(start):
            face_weights(
                d, keep.at[1], keep.at[2], keep.at[3], keep.at[4], keep.at[0], v,
                start, size, factor_x, my, mz, sy, sz,
            )

        def planes(u, start, amount):
            return stencil(
                u, keep.at[0], keep.at[1], keep.at[2], keep.at[3], start, amount, sy, sz
            )

        def smooth(start):
            for p, here, r in planes(v, start, count):
                keep[5, p] = here + keep[4, p] * r

        blocks(PAD, PAD + count, size, weights)
        blocks(PAD, PAD + count, count, smooth)
        return planes

    for g in range(X2 // 4):
        for f, ref in ((0, keep2.at[0]), (1, d2)):
            packed = [gathered[g, f, k] for k in range(3)]
            fourth = [pltpu.roll(packed[k], 32 * (k + 1), 1) for k in range(3)]
            fourth = jnp.where(lane < 32, fourth[0], jnp.where(lane < 64, fourth[1], fourth[2]))
            for k, plane in enumerate(packed + [fourth]):
                ref[PAD + 4 * g + k] = plane
    planes2 = level(keep2, d2, v2, X2, 32, 1, 1, 0.0625, ny // 4)

    def restrict(start):
        first = 2 * (start - PAD) + PAD
        res = [r for _, _, r in planes2(keep2.at[5], first, 32)]
        for i in range(16):
            total = res[2 * i] + res[2 * i + 1]
            keep3[0, start + i] = 0.125 * pair_rows(pair_lanes(total, 1), 1)
            total = d2[first + 2 * i] + d2[first + 2 * i + 1]
            d3[start + i] = 0.125 * pair_rows(pair_lanes(total, 1), 1)

    blocks(PAD, PAD + X3, 16, restrict)
    planes3 = level(keep3, d3, v3, X3, 32, 2, 2, 0.015625, ny // 4)

    def gather_pair(total):
        total = total + shift_down(total, 2, 1)
        return total + shift_down(total, 2, 0)

    res = [r for _, _, r in planes3(keep3.at[5], PAD, X3)]
    for i in range(X4):
        coarse[0, pl.ds(8 * i, 8), :] = gather_pair(res[2 * i] + res[2 * i + 1])
        coarse[1, pl.ds(8 * i, 8), :] = gather_pair(d3[PAD + 2 * i] + d3[PAD + 2 * i + 1])
    total = jnp.zeros((8, 128), F32)
    for g in range(8):
        f, s, half = g // 4, (g // 2) % 2, g % 2
        part = coarse[f, pl.ds(64 * half + 4 * s, 8, stride=8), :]
        part = pick_lanes(part, 16 + 4 * (lane % 16))
        total = jnp.where(lane // 16 == g, part, total)
    tile[...] = 0.125 * total


def coarsest(tiles):
    ngy = tiles.shape[0]
    width = 16 * ngy
    lane_group = iota((8, 128), 1) // 16
    fields = []
    for g in range(8):
        halves = []
        for h in range(width // 128):
            total = jnp.zeros((8, 128), F32)
            for q in range(8):
                piece = tiles[8 * h + q]
                shift = (16 * q - 16 * g) % 128
                if shift:
                    piece = pltpu.roll(piece, shift, 1)
                total = jnp.where(lane_group == q, piece, total)
            halves.append(total)
        fields.append(jnp.concatenate(halves, axis=1))
    whole = [jnp.concatenate([fields[2 * n], fields[2 * n + 1]], axis=0) for n in range(4)]
    shape = whole[0].shape
    factor = 2.0 * STEP * 0.25**4
    mx = jnp.where(iota(shape, 0) >= 1, F32(factor), F32(0.0))
    my = jnp.where(iota(shape, 1) >= 1, F32(factor), F32(0.0))
    out = []
    for s in range(2):
        b, d = whole[s], whole[2 + s]
        wx = mx * harm(d, shift_up(d, 1, 0))
        wy = my * harm(d, shift_up(d, 1, 1))
        inv = RELAX / (1.0 + (wx + shift_down(wx, 1, 0)) + (wy + shift_down(wy, 1, 1)))

        u = start = inv * b
        up_x, down_x = inv * wx, inv * shift_down(wx, 1, 0)
        up_y, down_y = inv * wy, inv * shift_down(wy, 1, 1)
        for _ in range(COARSE_SWEEPS - 1):
            along_x = up_x * shift_up(u, 1, 0) + down_x * shift_down(u, 1, 0)
            along_y = up_y * shift_up(u, 1, 1) + down_y * shift_down(u, 1, 1)
            u = ((1.0 - RELAX) * u + start) + (along_x + along_y)
        out.append(u + jnp.sum(b - u) / (shape[0] * shape[1]))
    return out


def up_kernel(
    tiles, keep2, keep3, keep0, keep1, react,
    out,
    c4, rep2, u3, u2, c2, p1, q1, q0,
):
    gx = lax.axis_index("gx")
    gy = lax.axis_index("gy")

    solved = jnp.concatenate(coarsest(tiles), axis=0)
    width = solved.shape[1]
    solved = pltpu.roll(solved, (width + 4 - 16 * gy) % width, 1)[:, :128]
    near = pick_lanes(solved, iota((1, 128), 1) // 4)
    for t in range(2):
        c4[t, pl.ds(0, 8), :] = jnp.zeros((8, 128), F32)
        c4[t, pl.ds(8, X4), :] = near[X4 * t : X4 * (t + 1)]
        c4[t, pl.ds(8 + X4, 8), :] = jnp.zeros((8, 128), F32)
    first_species = iota((8, 128), 0) < 4

    def coarse_plane(k):
        rows = [
            jnp.broadcast_to(c4[t, pl.ds(gx + 6 + k, 1), :], (8, 128)) for t in range(2)
        ]
        return jnp.where(first_species, rows[0], rows[1])

    def sweeps(keep, base, u, count, sy, sz):
        for turn in range(2):
            lo, hi = 1 + turn, count - 1 - turn
            here = u[lo]
            fx = keep[1, base + lo] * (here - u[lo - 1])
            for i in range(lo, hi):
                after = u[i + 1]
                fxn = keep[1, base + i + 1] * (after - here)
                r = residual_short(
                    here, keep[0, base + i], fx, fxn,
                    keep[2, base + i], keep[3, base + i], sy, sz,
                )
                u[i] = here + keep[4, base + i] * r
                here, fx = after, fxn

    base3 = gx * 2
    for i in range(0, 10, 2):
        plane = coarse_plane(i // 2)
        u3[i] = keep3[5, base3 + i] + plane
        u3[i + 1] = keep3[5, base3 + i + 1] + plane
    sweeps(keep3, base3, u3, 10, 2, 2)
    base2 = gx * 4
    for i in range(12):
        u2[i] = keep2[5, base2 + i] + u3[min(2 + i // 2, 9)]
    sweeps(keep2, base2, u2, 12, 1, 1)

    for i in range(8):
        for k in range(2):
            rep2[pl.ds(16 * i + k, 8, stride=2), :] = u2[2 + i]
    quarter = iota((1, 128), 1) // 4
    edge = jnp.where(quarter < 16, quarter + 80, quarter - 16)
    flat = [pick_lanes(rep2[...], lanes) for lanes in (quarter + 16, quarter + 48, edge)]
    flat = jnp.concatenate(flat, axis=1)
    c2[...] = flat.reshape(8, 2, 8, LN)

    def planes(keep, u, s, start, size, step):
        return stencil(
            u.at[s], keep.at[0, s], keep.at[1, s], keep.at[2, s], keep.at[3, s],
            start, size, step, 0 if step == 1 else 1,
        )

    def smooth(lo, hi, size, keep, u, new, step):
        def body(start):
            for s in range(2):
                for p, here, r in planes(keep, u, s, start, size, step):
                    new[s, p] = here + keep[4, s, p] * r

        blocks(lo, hi, size, body)

    for i in range(3, 17):
        for s in range(2):
            p1[s, i] = keep1[5, s, i] + c2[(i - 6) // 2 + 2, s]
    smooth(4, 16, 12, keep1, p1, q1, 2)
    smooth(5, 15, 10, keep1, q1, p1, 2)

    def corrected_sweep(n, carry):
        start = 3 + 6 * n
        for s in range(2):
            spread = [p1[s, 5 + 3 * n + j] for j in range(4)]
            spread = [jnp.concatenate([c, c], axis=0) for c in spread]
            u = [keep0[5, s, start - 1 + j] + spread[j // 2] for j in range(8)]
            fx = keep0[1, s, start] * (u[1] - u[0])
            for j in range(6):
                p = start + j
                fxn = keep0[1, s, p + 1] * (u[j + 2] - u[j + 1])
                r = residual(
                    u[j + 1], keep0[0, s, p], fx, fxn, keep0[2, s, p], keep0[3, s, p], 1, 0
                )
                q0[s, p] = u[j + 1] + keep0[4, s, p] * r
                fx = fxn
        return carry

    lax.fori_loop(0, 3, corrected_sweep, 0)

    def last(start):
        adj = [[], []]
        for s in range(2):
            for p, here, r in planes(keep0, q0, s, start, 4, 1):
                adj[s].append((here + keep0[4, s, p] * r)[:, :256])
        for j in range(4):
            x = start + j - HX
            a0, a1 = adj[0][j], adj[1][j]
            total = a0 + a1
            for s, value in enumerate((a0 - react[x, 1] * total, a1 - react[x, 0] * total)):
                out[s, :, 0, x, :] = value[:8]
                out[s, :, 1, x, :] = value[8:]

    blocks(4, 20, 4, last)


def call(
    kernel, outs, scratch, args, name, limit, kinds=None, aliases=None, cycles=0, dtypes=None
):
    spaces = {"v": pltpu.VMEM, "s": pltpu.SMEM}
    specs = [pl.BlockSpec(memory_space=spaces[k]) for k in kinds or "v" * len(args)]
    return pl.pallas_call(
        kernel,
        out_shape=[jax.ShapeDtypeStruct(o, d) for o, d in zip(outs, dtypes or [F32] * len(outs))],
        in_specs=specs,
        out_specs=[pl.BlockSpec(memory_space=pltpu.VMEM)] * len(outs),
        scratch_shapes=[pltpu.VMEM(s, F32) if isinstance(s, tuple) else s for s in scratch],
        input_output_aliases=aliases or {},
        compiler_params=pltpu.CompilerParams(vmem_limit_bytes=limit * 1024 * 1024),
        cost_estimate=pl.CostEstimate(flops=cycles, bytes_accessed=0, transcendentals=0)
        if cycles
        else None,
        name=name,
    )(*args)


def swap(axis, first, block):
    pairs = [(i, i + 1) for i in range(first, lax.axis_size(axis) - 1, 2)]
    return lax.ppermute(block, axis, pairs + [(j, i) for i, j in pairs])


def everyone(block, axis):
    count = lax.axis_size(axis)
    copies = jnp.broadcast_to(block[None], (count,) + block.shape)
    return lax.all_to_all(copies, axis, split_axis=0, concat_axis=0, tiled=True)


def per_device(counts, classes, diffusivity, cotangent):
    shape = cotangent.shape
    counts, cotangent = (a.reshape(2, 8, 2, 16, 256) for a in (counts, cotangent))
    classes = classes.reshape(8, 2, 16, 256)
    (table,) = call(table_kernel, [(16, 128)], [], (diffusivity,), "table", 8, "s", cycles=10**9)
    own, across, inside, table = call(
        turn_kernel,
        [(16, 3, 16, 256), (8, 3, 16, 128), (8, 3, 16, 128), (16, 128)], [],
        (cotangent, classes, table), "turn", 8,
    )
    across, inside = swap("gy", 1, across), swap("gy", 0, inside)
    strip = (3 * HX - 2, 16, 256)
    mfirst, msecond = call(cut_strips, [strip, strip], [], (own,), "strips", 8)
    mfirst, msecond = swap("gx", 1, mfirst), swap("gx", 0, msecond)
    strip = (3 * HX - 2, 16, 128)
    edge, sfirst, ssecond = call(
        edge_kernel, [(16, 3, 16, 128), strip, strip], [], (across, inside), "edge", 8
    )
    sfirst, ssecond = swap("gx", 1, sfirst), swap("gx", 0, ssecond)
    fine = [(6, 2, NPL, 16, LN), (6, 2, N1, 8, LN)]
    fine += [(2, NPL, 16, LN)] * 2 + [(2, N1, 8, LN)]
    kept = call(own_kernel, fine, [], (table, own, edge), "own", 8, cycles=10**7)
    strip = (9, 8, LN)
    first, second, keep0, keep1, _, _, d1 = call(
        near_kernel,
        [strip, strip] + fine, [],
        (table, mfirst, msecond, sfirst, ssecond, *kept), "near", 8,
        aliases={5 + n: 2 + n for n in range(5)},
    )
    first, second = swap("gx", 1, first), swap("gx", 0, second)
    level1 = [(6, 2, N1, 8, LN), (2, N1, 8, LN), (2, N1, 8, LN)]
    zs = (4, 16, 128)
    keep1, v1, react, diff2, matrix = call(
        inner_kernel, level1[:2] + [(16, 2, 16, 256), (3, 8, 128), (LN, 128)], [zs],
        (keep1, d1, counts), "inner", 8,
        aliases={0: 0}, cycles=10**7, dtypes=[F32] * 4 + [BF16],
    )
    message, keep1, _, _ = call(
        outer_kernel, [(2, 3, 8, 128)] + level1, [zs],
        (first, second, diff2, matrix, keep1, v1, d1), "outer", 8,
        aliases={4: 1, 5: 2, 6: 3},
    )
    gathered = everyone(message, "gx")
    tile, keep2, keep3 = call(
        middle_kernel,
        [(8, 128), (6, X2 + 2 * PAD, 8, 128), (6, X3 + 2 * PAD, 8, 128)],
        [(X2 + 2 * PAD, 8, 128), (X3 + 2 * PAD, 8, 128)] * 2 + [(2, 128, 128)],
        (gathered,), "middle", 8,
    )
    tiles = everyone(tile, "gy")
    (gradient,) = call(
        up_kernel,
        [(2, 8, 2, 16, 256)],
        [
            (2, X4 + 16, 128), (128, 128), (10, 8, 128), (12, 8, 128), (8, 2, 8, LN),
            (2, N1, 8, LN), (2, N1, 8, LN), (2, NPL, 16, LN),
        ],
        (tiles, keep2, keep3, keep0, keep1, react), "up", 12,
    )
    return gradient.reshape(shape)


def solution(mesh):
    in_specs = (P(None, None, "gx", "gy"), P(None, "gx", "gy"), P(), P(None, None, "gx", "gy"))
    out_specs = P(None, None, "gx", "gy")
    return jax.shard_map(
        per_device, mesh=mesh, in_specs=in_specs, out_specs=out_specs, check_vma=False
    )
```

```python
import jax
import jax.numpy as jnp
from jax import lax
from jax.experimental import pallas as pl
from jax.experimental.pallas import tpu as pltpu
from jax.sharding import PartitionSpec as P

F32 = jnp.float32
BF16 = jnp.bfloat16
RELAX = 0.8
REACT = 0.3
STEP = 256.0
COARSE_SWEEPS = 8

HX = 4
NPL = 16 + 2 * HX
N1 = 20
HY = 64
LN = 384
PAD = 4
X2 = 64
X3 = 32
X4 = 16


def iota(shape, axis):
    return lax.broadcasted_iota(jnp.int32, shape, axis)


def shift_up(value, by, axis):
    return pltpu.roll(value, by, axis)


def shift_down(value, by, axis):
    return pltpu.roll(value, value.shape[axis] - by, axis)


def reciprocal(x):
    return pl.reciprocal(x, approx=True)


def z_up(value, step):
    if step:
        return shift_up(value, step, 0)
    return jnp.concatenate([shift_up(value[8:], 1, 0), value[:8]], axis=0)


def z_down(value, step):
    if step:
        return shift_down(value, step, 0)
    return jnp.concatenate([value[8:], shift_down(value[:8], 1, 0)], axis=0)


def harm(a, b):
    return a * b * reciprocal(a + b)


def residual(u, b, fx, fxn, wy, wz, sy, sz):
    fy = wy * (u - shift_up(u, sy, 1))
    mu = u + (fx - fxn) + (fy - shift_down(fy, sy, 1))
    fz = wz * (u - z_up(u, sz))
    return b - (mu + (fz - z_down(fz, sz)))


def residual_short(u, b, fx, fxn, wy, wz, sy, sz):
    fy = wy * (u - shift_up(u, sy, 1)) - shift_down(wy, sy, 1) * (shift_down(u, sy, 1) - u)
    fz = wz * (u - z_up(u, sz)) - z_down(wz, sz) * (z_down(u, sz) - u)
    return b - (u + (fx - fxn) + (fy + fz))


def diagonal(wx, wxn, wy, wz, sy, sz):
    return 1.0 + (wx + wxn) + (wy + shift_down(wy, sy, 1)) + (wz + z_down(wz, sz))


def pair_lanes(value, half):
    width = value.shape[1]
    total = value + shift_down(value, half, 1)
    first = (iota(value.shape, 1) // half) % 2 == 0
    return jnp.where(first, total, shift_up(total, half, 1))


def pair_rows(value, half):
    total = value + shift_down(value, half, 0)
    first = (iota(value.shape, 0) // half) % 2 == 0
    return jnp.where(first, total, shift_up(total, half, 0))


def pick_lanes(value, lanes):
    return jnp.take_along_axis(value, jnp.broadcast_to(lanes, value.shape), axis=1)


def stencil(u, b, wx, wy, wz, start, count, sy, sz):
    here = u[start]
    fx = wx[start] * (here - u[start - 1])
    for j in range(count):
        p = start + j
        after = u[p + 1]
        fxn = wx[p + 1] * (after - here)
        yield p, here, residual(here, b[p], fx, fxn, wy[p], wz[p], sy, sz)
        here, fx = after, fxn


def face_weights(d, wx, wy, wz, inv, b, u, start, count, factor_x, my, mz, sy, sz):
    here = d[start]
    side = factor_x(start) * harm(here, d[start - 1])
    for j in range(count):
        p = start + j
        after = d[p + 1]
        siden = factor_x(p + 1) * harm(after, here)
        y = my * harm(here, shift_up(here, sy, 1))
        z = mz * harm(here, z_up(here, sz))
        wx[p], wy[p], wz[p] = side, y, z
        value = RELAX * reciprocal(diagonal(side, siden, y, z, sy, sz))
        inv[p] = value
        u[p] = value * b[p]
        here, side = after, siden


def blocks(lo, hi, size, body):
    assert (hi - lo) % size == 0
    if hi - lo == size:
        body(lo)
        return

    def step(n, carry):
        body(lo + n * size)
        return carry

    lax.fori_loop(0, (hi - lo) // size, step, 0)


def table_kernel(diff_ref, table):
    for s in range(2):
        for c in range(8):
            table[pl.ds(8 * s + c, 1), :] = jnp.full((1, 128), diff_ref[s, c], F32)


def first_kernel(out):
    out[...] = jnp.zeros((8, 128), F32)


def turn_kernel(cot, cls, start, own, across, inside):
    odd = lax.axis_index("gy") % 2 == 1
    left_half = iota((16, 128), 1) < HY
    for f in range(3):
        for k in range(8):
            pair = []
            for x in (k, k + 8):
                halves = [cls[:, n, x, :] if f == 2 else cot[f, :, n, x, :] for n in range(2)]
                pair.append(jnp.concatenate(halves, axis=0).astype(F32))
                own[x, f] = pair[-1]
            a, b = pair
            to_left = jnp.where(left_half, a[:, :128], pltpu.roll(b[:, :128], HY, 1))
            to_right = jnp.where(left_half, pltpu.roll(b[:, 128:], HY, 1), a[:, 128:])
            across[k, f] = jnp.where(odd, to_right, to_left)
            inside[k, f] = jnp.where(odd, to_left, to_right)


def cut_strips(planes, first, second):
    odd = lax.axis_index("gx") % 2 == 1
    for f in range(3):
        place = 0 if f == 2 else HX + f * (HX - 1)
        count = HX if f == 2 else HX - 1
        for n in range(count):
            low, high = planes[n, f], planes[16 - count + n, f]
            first[place + n] = jnp.where(odd, high, low)
            second[place + n] = jnp.where(odd, low, high)


def edge_kernel(across, inside, edge, first, second):
    odd = lax.axis_index("gy") % 2 == 1
    left_half = iota((16, 128), 1) < HY
    for k in range(8):
        for f in range(3):
            got = across[k, f], inside[k, f]
            fl, fr = jnp.where(odd, got[1], got[0]), jnp.where(odd, got[0], got[1])
            edge[k, f] = jnp.where(left_half, fr, fl)
            edge[k + 8, f] = pltpu.roll(jnp.where(left_half, fl, fr), HY, 1)
    cut_strips(edge, first, second)


def fine_tools(table, keep0, keep1, d0, v0, d1):
    gx = lax.axis_index("gx")
    gy = lax.axis_index("gy")
    nx = 16 * lax.axis_size("gx")
    ny = 256 * lax.axis_size("gy")
    b0, u0, b1 = keep0[0], keep0[5], keep1[0]

    def look_up(values):
        cls = values.astype(jnp.int32)
        bits = [(cls & (1 << n)) != 0 for n in range(3)]
        out = []
        for s in range(2):
            rows = [jnp.broadcast_to(table[pl.ds(8 * s + c, 1), :], (16, 128)) for c in range(8)]
            rows = [jnp.concatenate([r] * (cls.shape[1] // 128), axis=1) for r in rows]
            rows = [jnp.where(bits[0], rows[2 * n + 1], rows[2 * n]) for n in range(4)]
            rows = [jnp.where(bits[1], rows[2 * n + 1], rows[2 * n]) for n in range(2)]
            out.append(jnp.where(bits[2], rows[1], rows[0]))
        return out

    def assemble_own(own, edge, size):
        def body(start):
            for j in range(size):
                x = start + j
                planes = [jnp.concatenate([own[x, f], edge[x, f]], axis=1) for f in range(3)]
                for s, d in enumerate(look_up(planes[2])):
                    b0[s, x + HX] = planes[s]
                    d0[s, x + HX] = d

        blocks(0, 16, size, body)

    def assemble_strip(strips, high, cut):
        second = (gx + high) % 2 == 1

        def plane(n):
            return jnp.where(second, strips[1][n], strips[0][n])

        lo = 20 * high
        for j in range(HX):
            for s, d in enumerate(look_up(plane(j))):
                d0[s, lo + j, :, cut] = d
        for s in range(2):
            for n in range(HX - 1):
                b0[s, lo + 1 - high + n, :, cut] = plane(HX + s * (HX - 1) + n)

    def masks(rows, step, factor, origin):
        lane = iota((rows, LN), 1)
        ypos = gy * 256 + jnp.where(lane < 256 + HY, lane, lane - LN)
        my = jnp.where((ypos >= step) & (ypos < ny), F32(factor), F32(0.0))
        mz = jnp.where(iota((rows, LN), 0) >= 1, F32(factor), F32(0.0))

        def factor_x(p):
            xpos = (gx * 16) // step + p - origin
            return jnp.where((xpos >= 1) & (xpos < nx // step), F32(factor), F32(0.0))

        return my, mz, factor_x

    def weigh(lo, hi, size, rows, step, factor, d, keep, v):
        blocks(lo, hi, size, weigher(size, rows, step, factor, d, keep, v))

    def weigher(size, rows, step, factor, d, keep, v):
        my, mz, factor_x = masks(rows, step, factor, HX if step == 1 else 6)

        def body(start):
            for s in range(2):
                face_weights(
                    d.at[s], keep[1].at[s], keep[2].at[s], keep[3].at[s], keep[4].at[s],
                    keep[0].at[s], v.at[s], start, size, factor_x, my, mz, step, 0 if step == 1 else 1,
                )

        return body

    def planes(keep, u, s, start, size, step):
        return stencil(
            u.at[s], keep[0].at[s], keep[1].at[s], keep[2].at[s], keep[3].at[s],
            start, size, step, 0 if step == 1 else 1,
        )

    def smooth(lo, hi, size, keep, v, step):
        blocks(lo, hi, size, smoother(size, keep, v, step))

    def smoother(size, keep, v, step):
        def body(start):
            for s in range(2):
                for p, here, r in planes(keep, v, s, start, size, step):
                    keep[5][s, p] = here + keep[4][s, p] * r

        return body

    def restrict(lo, hi, size):
        blocks(lo, hi, size, restricter(size))

    def restricter(size):
        def body(start):
            for s in range(2):
                res = [r for _, _, r in planes(keep0, u0, s, 2 * start - 8, 2 * size, 1)]
                for i in range(size):
                    total = res[2 * i] + res[2 * i + 1]
                    b1[s, start + i] = 0.125 * pair_lanes(total[:8] + total[8:], 1)

        return body

    def coarse_diff(lo, hi, size):
        def body(start):
            for i in range(size):
                for s in range(2):
                    p = 2 * (start + i) - 8
                    total = d0[s, p] + d0[s, p + 1]
                    d1[s, start + i] = 0.125 * pair_lanes(total[:8] + total[8:], 1)

        blocks(lo, hi, size, body)

    at = assemble_strip, weigher, smoother, restricter
    return assemble_own, at, weigh, smooth, restrict, coarse_diff, planes


FINE = 2.0 * STEP
COARSER = 0.5 * STEP


def own_kernel(table, own, edge, mfirst, msecond, *refs):
    keep0, keep1, (d0, v0, d1) = refs[:6], refs[6:12], refs[12:]
    assemble_own, at, weigh, smooth, restrict, coarse_diff, _ = fine_tools(
        table, keep0, keep1, d0, v0, d1
    )

    def one_side(high, carry):
        at[0]((mfirst, msecond), high, slice(0, 256))
        return carry

    lax.fori_loop(0, 2, one_side, 0)
    assemble_own(own, edge, 4)
    weigh(5, 19, 7, 16, 1, FINE, d0, keep0, v0)
    smooth(6, 18, 4, keep0, v0, 1)
    restrict(8, 12, 2)
    coarse_diff(6, 14, 4)


def near_kernel(
    table, sfirst, ssecond, *refs,
):
    first, second, *refs = refs[15:]
    keep0, keep1, (d0, v0, d1) = refs[:6], refs[6:12], refs[12:]
    _, at, _, _, _, _, _ = fine_tools(table, keep0, keep1, d0, v0, d1)
    assemble_strip, weigher, smoother, restricter = at
    weigh = weigher(4, 16, 1, FINE, d0, keep0, v0)
    smooth = smoother(4, keep0, v0, 1)
    restrict = restricter(2)

    def one_side(high, carry):
        assemble_strip((sfirst, ssecond), high, slice(256, LN))
        weigh(1 + 18 * high)
        smooth(2 + 16 * high)
        restrict(6 + 6 * high)
        return carry

    lax.fori_loop(0, 2, one_side, 0)
    odd = lax.axis_index("gx") % 2 == 1
    even_lane = iota((8, LN), 1) % 2 == 0

    def send(n, ref, low, high):
        low, high = (jnp.where(even_lane, ref[0, m], ref[1, m]) for m in (low, high))
        first[n] = jnp.where(odd, high, low)
        second[n] = jnp.where(odd, low, high)

    for k in range(4):
        send(k, keep1[0], 6 + k, 10 + k)
    for k in range(5):
        send(4 + k, d1, 6 + k, 9 + k)


def averaging(shape, dtype):
    group = iota(shape, 0) // 4
    target = jnp.where(group < (256 + HY) // 4, group + 16, group - 80)
    return jnp.where(iota(shape, 1) == target, F32(0.0625), F32(0.0)).astype(dtype)


def to_level2(rows, matrix, zs, message):
    rows = jnp.concatenate(rows, axis=0)
    high = rows.astype(BF16)
    rest = rows - high.astype(F32)
    middle = rest.astype(BF16)
    low = (rest - middle.astype(F32)).astype(BF16)
    whole = jnp.dot(
        jnp.concatenate([high, middle, low], axis=0), matrix, preferred_element_type=F32
    )
    whole = whole[0:64] + whole[64:128] + whole[128:192]
    lane = iota((8, 128), 1)
    halved = []
    for n in range(4):
        part = zs.at[n]
        part[...] = whole[16 * n : 16 * (n + 1)]
        halved.append(part[pl.ds(0, 8, stride=2), :] + part[pl.ds(1, 8, stride=2), :])
    for k in range(3):
        message[k] = jnp.where(lane < 96, halved[k], pltpu.roll(halved[3], 96 - 32 * k, 1))


def inner_kernel(d1, counts, *refs):
    keep1, (v1, react, diff2, matrix, zs) = refs[6:12], refs[12:]
    _, _, weigh, smooth, _, _, _ = fine_tools(None, keep1, keep1, None, None, d1)
    weigh(7, 13, 6, 8, 2, COARSER, d1, keep1, v1)
    smooth(8, 12, 4, keep1, v1, 2)
    for s in range(2):
        for x in range(16):
            halves = [counts[s, :, n, x, :] for n in range(2)]
            react[x, s] = REACT * (0.25 * jnp.concatenate(halves, axis=0).astype(F32))
    matrix[...] = averaging((LN, 128), BF16)
    rows = [d1[s, 6 + 2 * n] + d1[s, 7 + 2 * n] for n in range(4) for s in range(2)]
    to_level2(rows, matrix[...], zs, diff2)


def outer_kernel(first, second, diff2, matrix, *refs):
    message, *refs = refs[8:]
    keep1, (v1, d1, zs) = refs[:6], refs[6:]
    _, _, weigh, smooth, _, _, planes = fine_tools(None, keep1, keep1, None, None, d1)
    gx = lax.axis_index("gx")
    last = lax.axis_size("gx") - 1
    odd = gx % 2 == 1
    even_lane = iota((8, LN), 1) % 2 == 0

    def both(got, ref, m, real=None):
        if real is not None:
            got = jnp.where(real, got, F32(1.0))
        ref[0, m] = jnp.where(even_lane, got, shift_up(got, 1, 1))
        ref[1, m] = jnp.where(even_lane, shift_down(got, 1, 1), got)

    for k in range(9):
        low = jnp.where(odd, second[k], first[k])
        high = jnp.where(odd, first[k], second[k])
        if k < 4:
            both(low, keep1[0], 2 + k)
            both(high, keep1[0], 14 + k)
        else:
            both(low, d1, k - 3, gx > 0)
            both(high, d1, 10 + k, gx < last)
    for start in (2, 13):
        weigh(start, start + 5, 5, 8, 2, COARSER, d1, keep1, v1)
    for start in (3, 12):
        smooth(start, start + 5, 5, keep1, v1, 2)
    res = [[r for _, _, r in planes(keep1, keep1[5], s, 6, 8, 2)] for s in range(2)]
    rows = [res[s][2 * n] + res[s][2 * n + 1] for n in range(4) for s in range(2)]
    to_level2(rows, matrix[...], zs, message.at[0])
    message[1] = diff2[...]


def middle_kernel(gathered, tile, keep2, keep3, d2, d3, v2, v3, coarse):
    gy = lax.axis_index("gy")
    ny = 256 * lax.axis_size("gy")
    lane = iota((8, 128), 1)
    row = iota((8, 128), 0)
    ypos = gy * 64 + lane - 16
    zero = jnp.zeros((8, 128), F32)

    for keep, d, v, count in ((keep2, d2, v2, X2), (keep3, d3, v3, X3)):
        for k in range(PAD):
            for n in range(6):
                keep[n, k] = zero
                keep[n, count + PAD + k] = zero
        for p in (PAD - 1, PAD + count):
            d[p] = zero + 1.0
            v[p] = zero

    def level(keep, d, v, count, size, sy, sz, scale, nyl):
        factor = 2.0 * STEP * scale
        my = jnp.where((ypos >= sy) & (ypos < nyl), F32(factor), F32(0.0))
        mz = jnp.where(row % 4 >= sz, F32(factor), F32(0.0))

        def factor_x(p):
            return jnp.where((p > PAD) & (p < PAD + count), F32(factor), F32(0.0))

        def weights(start):
            face_weights(
                d, keep.at[1], keep.at[2], keep.at[3], keep.at[4], keep.at[0], v,
                start, size, factor_x, my, mz, sy, sz,
            )

        def planes(u, start, amount):
            return stencil(
                u, keep.at[0], keep.at[1], keep.at[2], keep.at[3], start, amount, sy, sz
            )

        def smooth(start):
            for p, here, r in planes(v, start, count):
                keep[5, p] = here + keep[4, p] * r

        blocks(PAD, PAD + count, size, weights)
        blocks(PAD, PAD + count, count, smooth)
        return planes

    for g in range(X2 // 4):
        for f, ref in ((0, keep2.at[0]), (1, d2)):
            packed = [gathered[g, f, k] for k in range(3)]
            fourth = [pltpu.roll(packed[k], 32 * (k + 1), 1) for k in range(3)]
            fourth = jnp.where(lane < 32, fourth[0], jnp.where(lane < 64, fourth[1], fourth[2]))
            for k, plane in enumerate(packed + [fourth]):
                ref[PAD + 4 * g + k] = plane
    planes2 = level(keep2, d2, v2, X2, 32, 1, 1, 0.0625, ny // 4)

    def restrict(start):
        first = 2 * (start - PAD) + PAD
        res = [r for _, _, r in planes2(keep2.at[5], first, 32)]
        for i in range(16):
            total = res[2 * i] + res[2 * i + 1]
            keep3[0, start + i] = 0.125 * pair_rows(pair_lanes(total, 1), 1)
            total = d2[first + 2 * i] + d2[first + 2 * i + 1]
            d3[start + i] = 0.125 * pair_rows(pair_lanes(total, 1), 1)

    blocks(PAD, PAD + X3, 16, restrict)
    planes3 = level(keep3, d3, v3, X3, 32, 2, 2, 0.015625, ny // 4)

    def gather_pair(total):
        total = total + shift_down(total, 2, 1)
        return total + shift_down(total, 2, 0)

    res = [r for _, _, r in planes3(keep3.at[5], PAD, X3)]
    for i in range(X4):
        coarse[0, pl.ds(8 * i, 8), :] = gather_pair(res[2 * i] + res[2 * i + 1])
        coarse[1, pl.ds(8 * i, 8), :] = gather_pair(d3[PAD + 2 * i] + d3[PAD + 2 * i + 1])
    total = jnp.zeros((8, 128), F32)
    for g in range(8):
        f, s, half = g // 4, (g // 2) % 2, g % 2
        part = coarse[f, pl.ds(64 * half + 4 * s, 8, stride=8), :]
        part = pick_lanes(part, 16 + 4 * (lane % 16))
        total = jnp.where(lane // 16 == g, part, total)
    tile[...] = 0.125 * total


def coarsest(tiles):
    ngy = tiles.shape[0]
    width = 16 * ngy
    lane_group = iota((8, 128), 1) // 16
    fields = []
    for g in range(8):
        halves = []
        for h in range(width // 128):
            total = jnp.zeros((8, 128), F32)
            for q in range(8):
                piece = tiles[8 * h + q]
                shift = (16 * q - 16 * g) % 128
                if shift:
                    piece = pltpu.roll(piece, shift, 1)
                total = jnp.where(lane_group == q, piece, total)
            halves.append(total)
        fields.append(jnp.concatenate(halves, axis=1))
    whole = [jnp.concatenate([fields[2 * n], fields[2 * n + 1]], axis=0) for n in range(4)]
    shape = whole[0].shape
    factor = 2.0 * STEP * 0.25**4
    mx = jnp.where(iota(shape, 0) >= 1, F32(factor), F32(0.0))
    my = jnp.where(iota(shape, 1) >= 1, F32(factor), F32(0.0))
    out = []
    for s in range(2):
        b, d = whole[s], whole[2 + s]
        wx = mx * harm(d, shift_up(d, 1, 0))
        wy = my * harm(d, shift_up(d, 1, 1))
        inv = RELAX / (1.0 + (wx + shift_down(wx, 1, 0)) + (wy + shift_down(wy, 1, 1)))

        u = start = inv * b
        up_x, down_x = inv * wx, inv * shift_down(wx, 1, 0)
        up_y, down_y = inv * wy, inv * shift_down(wy, 1, 1)
        for _ in range(COARSE_SWEEPS - 1):
            along_x = up_x * shift_up(u, 1, 0) + down_x * shift_down(u, 1, 0)
            along_y = up_y * shift_up(u, 1, 1) + down_y * shift_down(u, 1, 1)
            u = ((1.0 - RELAX) * u + start) + (along_x + along_y)
        out.append(u + jnp.sum(b - u) / (shape[0] * shape[1]))
    return out


def up_kernel(
    tiles, keep2, keep3, react, *refs,
):
    keep0, keep1, (out, c4, rep2, u3, u2, c2, p1, q1, q0) = refs[:6], refs[6:12], refs[12:]
    gx = lax.axis_index("gx")
    gy = lax.axis_index("gy")

    solved = jnp.concatenate(coarsest(tiles), axis=0)
    width = solved.shape[1]
    solved = pltpu.roll(solved, (width + 4 - 16 * gy) % width, 1)[:, :128]
    near = pick_lanes(solved, iota((1, 128), 1) // 4)
    for t in range(2):
        c4[t, pl.ds(0, 8), :] = jnp.zeros((8, 128), F32)
        c4[t, pl.ds(8, X4), :] = near[X4 * t : X4 * (t + 1)]
        c4[t, pl.ds(8 + X4, 8), :] = jnp.zeros((8, 128), F32)
    first_species = iota((8, 128), 0) < 4

    def coarse_plane(k):
        rows = [
            jnp.broadcast_to(c4[t, pl.ds(gx + 6 + k, 1), :], (8, 128)) for t in range(2)
        ]
        return jnp.where(first_species, rows[0], rows[1])

    def sweeps(keep, base, u, count, sy, sz):
        for turn in range(2):
            lo, hi = 1 + turn, count - 1 - turn
            here = u[lo]
            fx = keep[1, base + lo] * (here - u[lo - 1])
            for i in range(lo, hi):
                after = u[i + 1]
                fxn = keep[1, base + i + 1] * (after - here)
                r = residual_short(
                    here, keep[0, base + i], fx, fxn,
                    keep[2, base + i], keep[3, base + i], sy, sz,
                )
                u[i] = here + keep[4, base + i] * r
                here, fx = after, fxn

    base3 = gx * 2
    for i in range(0, 10, 2):
        plane = coarse_plane(i // 2)
        u3[i] = keep3[5, base3 + i] + plane
        u3[i + 1] = keep3[5, base3 + i + 1] + plane
    sweeps(keep3, base3, u3, 10, 2, 2)
    base2 = gx * 4
    for i in range(12):
        u2[i] = keep2[5, base2 + i] + u3[min(2 + i // 2, 9)]
    sweeps(keep2, base2, u2, 12, 1, 1)

    for i in range(8):
        for k in range(2):
            rep2[pl.ds(16 * i + k, 8, stride=2), :] = u2[2 + i]
    quarter = iota((1, 128), 1) // 4
    edge = jnp.where(quarter < 16, quarter + 80, quarter - 16)
    flat = [pick_lanes(rep2[...], lanes) for lanes in (quarter + 16, quarter + 48, edge)]
    flat = jnp.concatenate(flat, axis=1)
    c2[...] = flat.reshape(8, 2, 8, LN)

    def planes(keep, u, s, start, size, step):
        return stencil(
            u.at[s], keep[0].at[s], keep[1].at[s], keep[2].at[s], keep[3].at[s],
            start, size, step, 0 if step == 1 else 1,
        )

    def smooth(lo, hi, size, keep, u, new, step):
        def body(start):
            for s in range(2):
                for p, here, r in planes(keep, u, s, start, size, step):
                    new[s, p] = here + keep[4][s, p] * r

        blocks(lo, hi, size, body)

    for i in range(3, 17):
        for s in range(2):
            p1[s, i] = keep1[5][s, i] + c2[(i - 6) // 2 + 2, s]
    smooth(4, 16, 12, keep1, p1, q1, 2)
    smooth(5, 15, 10, keep1, q1, p1, 2)

    def corrected_sweep(n, carry):
        start = 3 + 6 * n
        for s in range(2):
            spread = [p1[s, 5 + 3 * n + j] for j in range(4)]
            spread = [jnp.concatenate([c, c], axis=0) for c in spread]
            u = [keep0[5][s, start - 1 + j] + spread[j // 2] for j in range(8)]
            fx = keep0[1][s, start] * (u[1] - u[0])
            for j in range(6):
                p = start + j
                fxn = keep0[1][s, p + 1] * (u[j + 2] - u[j + 1])
                r = residual(
                    u[j + 1], keep0[0][s, p], fx, fxn, keep0[2][s, p], keep0[3][s, p], 1, 0
                )
                q0[s, p] = u[j + 1] + keep0[4][s, p] * r
                fx = fxn
        return carry

    lax.fori_loop(0, 3, corrected_sweep, 0)

    def last(start):
        adj = [[], []]
        for s in range(2):
            for p, here, r in planes(keep0, q0, s, start, 4, 1):
                adj[s].append((here + keep0[4][s, p] * r)[:, :256])
        for j in range(4):
            x = start + j - HX
            a0, a1 = adj[0][j], adj[1][j]
            total = a0 + a1
            for s, value in enumerate((a0 - react[x, 1] * total, a1 - react[x, 0] * total)):
                out[s, :, 0, x, :] = value[:8]
                out[s, :, 1, x, :] = value[8:]

    blocks(4, 20, 4, last)


def call(
    kernel, outs, scratch, args, name, limit, kinds=None, aliases=None, cycles=0, dtypes=None
):
    spaces = {"v": pltpu.VMEM, "s": pltpu.SMEM}
    specs = [pl.BlockSpec(memory_space=spaces[k]) for k in kinds or "v" * len(args)]
    return pl.pallas_call(
        kernel,
        out_shape=[jax.ShapeDtypeStruct(o, d) for o, d in zip(outs, dtypes or [F32] * len(outs))],
        in_specs=specs,
        out_specs=[pl.BlockSpec(memory_space=pltpu.VMEM)] * len(outs),
        scratch_shapes=[pltpu.VMEM(s, F32) if isinstance(s, tuple) else s for s in scratch],
        input_output_aliases=aliases or {},
        compiler_params=pltpu.CompilerParams(vmem_limit_bytes=limit * 1024 * 1024),
        cost_estimate=pl.CostEstimate(flops=cycles, bytes_accessed=0, transcendentals=0)
        if cycles
        else None,
        name=name,
    )(*args)


def swap(axis, first, block):
    pairs = [(i, i + 1) for i in range(first, lax.axis_size(axis) - 1, 2)]
    return lax.ppermute(block, axis, pairs + [(j, i) for i, j in pairs])


def everyone(block, axis):
    count = lax.axis_size(axis)
    copies = jnp.broadcast_to(block[None], (count,) + block.shape)
    return lax.all_to_all(copies, axis, split_axis=0, concat_axis=0, tiled=True)


def per_device(counts, classes, diffusivity, cotangent):
    shape = cotangent.shape
    counts, cotangent = (a.reshape(2, 8, 2, 16, 256) for a in (counts, cotangent))
    classes = classes.reshape(8, 2, 16, 256)
    (start,) = call(first_kernel, [(8, 128)], [], (), "first", 8, cycles=10**9)
    (table,) = call(table_kernel, [(16, 128)], [], (diffusivity,), "table", 8, "s")
    own, across, inside = call(
        turn_kernel,
        [(16, 3, 16, 256), (8, 3, 16, 128), (8, 3, 16, 128)], [],
        (cotangent, classes, start), "turn", 8,
    )
    across, inside = swap("gy", 1, across), swap("gy", 0, inside)
    strip = (3 * HX - 2, 16, 256)
    mfirst, msecond = call(cut_strips, [strip, strip], [], (own,), "strips", 8)
    mfirst, msecond = swap("gx", 1, mfirst), swap("gx", 0, msecond)
    strip = (3 * HX - 2, 16, 128)
    edge, sfirst, ssecond = call(
        edge_kernel, [(16, 3, 16, 128), strip, strip], [], (across, inside), "edge", 8
    )
    sfirst, ssecond = swap("gx", 1, sfirst), swap("gx", 0, ssecond)
    level0, level1 = (2, NPL, 16, LN), (2, N1, 8, LN)
    fine = [level0] * 6 + [level1] * 6 + [level0] * 2 + [level1]
    kept = call(own_kernel, fine, [], (table, own, edge, mfirst, msecond), "own", 8, cycles=10**7)
    strip = (9, 8, LN)
    first, second, *kept = call(
        near_kernel,
        [strip, strip] + fine, [],
        (table, sfirst, ssecond, *kept), "near", 8,
        aliases={3 + n: 2 + n for n in range(15)},
    )
    keep0, keep1, d1 = kept[:6], kept[6:12], kept[14]
    first, second = swap("gx", 1, first), swap("gx", 0, second)
    zs = (4, 16, 128)
    *keep1, v1, react, diff2, matrix = call(
        inner_kernel, [level1] * 7 + [(16, 2, 16, 256), (3, 8, 128), (LN, 128)], [zs],
        (d1, counts, *keep1), "inner", 8,
        aliases={2 + n: n for n in range(6)}, cycles=10**7, dtypes=[F32] * 9 + [BF16],
    )
    message, *keep1, _, _ = call(
        outer_kernel, [(2, 3, 8, 128)] + [level1] * 8, [zs],
        (first, second, diff2, matrix, *keep1, v1, d1), "outer", 8,
        aliases={4 + n: 1 + n for n in range(8)},
    )
    gathered = everyone(message, "gx")
    tile, keep2, keep3 = call(
        middle_kernel,
        [(8, 128), (6, X2 + 2 * PAD, 8, 128), (6, X3 + 2 * PAD, 8, 128)],
        [(X2 + 2 * PAD, 8, 128), (X3 + 2 * PAD, 8, 128)] * 2 + [(2, 128, 128)],
        (gathered,), "middle", 8,
    )
    tiles = everyone(tile, "gy")
    (gradient,) = call(
        up_kernel,
        [(2, 8, 2, 16, 256)],
        [
            (2, X4 + 16, 128), (128, 128), (10, 8, 128), (12, 8, 128), (8, 2, 8, LN),
            (2, N1, 8, LN), (2, N1, 8, LN), (2, NPL, 16, LN),
        ],
        (tiles, keep2, keep3, react, *keep0, *keep1), "up", 12,
    )
    return gradient.reshape(shape)


def solution(mesh):
    in_specs = (P(None, None, "gx", "gy"), P(None, "gx", "gy"), P(), P(None, None, "gx", "gy"))
    out_specs = P(None, None, "gx", "gy")
    return jax.shard_map(
        per_device, mesh=mesh, in_specs=in_specs, out_specs=out_specs, check_vma=False
    )
```

```python
import jax
import jax.numpy as jnp
from jax import lax
from jax.experimental import pallas as pl
from jax.experimental.pallas import tpu as pltpu
from jax.sharding import PartitionSpec as P

F32 = jnp.float32
BF16 = jnp.bfloat16
RELAX = 0.8
REACT = 0.3
STEP = 256.0
COARSE_SWEEPS = 8

HX = 4
NPL = 16 + 2 * HX
N1 = 20
HY = 64
LN = 384
PAD = 4
X2 = 64
X3 = 32
X4 = 16


def iota(shape, axis):
    return lax.broadcasted_iota(jnp.int32, shape, axis)


def shift_up(value, by, axis):
    return pltpu.roll(value, by, axis)


def shift_down(value, by, axis):
    return pltpu.roll(value, value.shape[axis] - by, axis)


def reciprocal(x):
    return pl.reciprocal(x, approx=True)


def z_up(value, step):
    if step:
        return shift_up(value, step, 0)
    return jnp.concatenate([shift_up(value[8:], 1, 0), value[:8]], axis=0)


def z_down(value, step):
    if step:
        return shift_down(value, step, 0)
    return jnp.concatenate([value[8:], shift_down(value[:8], 1, 0)], axis=0)


def harm(a, b):
    return a * b * reciprocal(a + b)


def residual(u, b, fx, fxn, wy, wz, sy, sz):
    fy = wy * (u - shift_up(u, sy, 1))
    mu = u + (fx - fxn) + (fy - shift_down(fy, sy, 1))
    fz = wz * (u - z_up(u, sz))
    return b - (mu + (fz - z_down(fz, sz)))


def residual_short(u, b, fx, fxn, wy, wz, sy, sz):
    fy = wy * (u - shift_up(u, sy, 1)) - shift_down(wy, sy, 1) * (shift_down(u, sy, 1) - u)
    fz = wz * (u - z_up(u, sz)) - z_down(wz, sz) * (z_down(u, sz) - u)
    return b - (u + (fx - fxn) + (fy + fz))


def diagonal(wx, wxn, wy, wz, sy, sz):
    return 1.0 + (wx + wxn) + (wy + shift_down(wy, sy, 1)) + (wz + z_down(wz, sz))


def pair_lanes(value, half):
    width = value.shape[1]
    total = value + shift_down(value, half, 1)
    first = (iota(value.shape, 1) // half) % 2 == 0
    return jnp.where(first, total, shift_up(total, half, 1))


def pair_rows(value, half):
    total = value + shift_down(value, half, 0)
    first = (iota(value.shape, 0) // half) % 2 == 0
    return jnp.where(first, total, shift_up(total, half, 0))


def pick_lanes(value, lanes):
    return jnp.take_along_axis(value, jnp.broadcast_to(lanes, value.shape), axis=1)


def stencil(u, b, wx, wy, wz, start, count, sy, sz):
    here = u[start]
    fx = wx[start] * (here - u[start - 1])
    for j in range(count):
        p = start + j
        after = u[p + 1]
        fxn = wx[p + 1] * (after - here)
        yield p, here, residual(here, b[p], fx, fxn, wy[p], wz[p], sy, sz)
        here, fx = after, fxn


def face_weights(d, wx, wy, wz, inv, b, u, start, count, factor_x, my, mz, sy, sz):
    here = d[start]
    side = factor_x(start) * harm(here, d[start - 1])
    for j in range(count):
        p = start + j
        after = d[p + 1]
        siden = factor_x(p + 1) * harm(after, here)
        y = my * harm(here, shift_up(here, sy, 1))
        z = mz * harm(here, z_up(here, sz))
        wx[p], wy[p], wz[p] = side, y, z
        value = RELAX * reciprocal(diagonal(side, siden, y, z, sy, sz))
        inv[p] = value
        u[p] = value * b[p]
        here, side = after, siden


def blocks(lo, hi, size, body):
    assert (hi - lo) % size == 0
    if hi - lo == size:
        body(lo)
        return

    def step(n, carry):
        body(lo + n * size)
        return carry

    lax.fori_loop(0, (hi - lo) // size, step, 0)


def table_kernel(diff_ref, table):
    for s in range(2):
        for c in range(8):
            value = diff_ref[pl.ds(s, 1), pl.ds(c, 1)]
            table[pl.ds(8 * s + c, 1), :] = jnp.broadcast_to(value, (1, 128))


def first_kernel(out):
    out[...] = jnp.zeros((8, 128), F32)


def turn_kernel(cot, cls, start, own, across, inside):
    odd = lax.axis_index("gy") % 2 == 1
    left_half = iota((16, 128), 1) < HY
    for f in range(3):
        for k in range(8):
            pair = []
            for x in (k, k + 8):
                halves = [cls[:, n, x, :] if f == 2 else cot[f, :, n, x, :] for n in range(2)]
                pair.append(jnp.concatenate(halves, axis=0).astype(F32))
                own[x, f] = pair[-1]
            a, b = pair
            to_left = jnp.where(left_half, a[:, :128], pltpu.roll(b[:, :128], HY, 1))
            to_right = jnp.where(left_half, pltpu.roll(b[:, 128:], HY, 1), a[:, 128:])
            across[k, f] = jnp.where(odd, to_right, to_left)
            inside[k, f] = jnp.where(odd, to_left, to_right)


def cut_strips(planes, first, second):
    odd = lax.axis_index("gx") % 2 == 1
    for f in range(3):
        place = 0 if f == 2 else HX + f * (HX - 1)
        count = HX if f == 2 else HX - 1
        for n in range(count):
            low, high = planes[n, f], planes[16 - count + n, f]
            first[place + n] = jnp.where(odd, high, low)
            second[place + n] = jnp.where(odd, low, high)


def edge_kernel(across, inside, edge, first, second):
    odd = lax.axis_index("gy") % 2 == 1
    left_half = iota((16, 128), 1) < HY
    for k in range(8):
        for f in range(3):
            got = across[k, f], inside[k, f]
            fl, fr = jnp.where(odd, got[1], got[0]), jnp.where(odd, got[0], got[1])
            edge[k, f] = jnp.where(left_half, fr, fl)
            edge[k + 8, f] = pltpu.roll(jnp.where(left_half, fl, fr), HY, 1)
    cut_strips(edge, first, second)


def fine_tools(table, keep0, keep1, d0, v0, d1):
    gx = lax.axis_index("gx")
    gy = lax.axis_index("gy")
    nx = 16 * lax.axis_size("gx")
    ny = 256 * lax.axis_size("gy")
    b0, u0, b1 = keep0[0], keep0[5], keep1[0]

    def look_up(values):
        cls = values.astype(jnp.int32)
        bits = [(cls & (1 << n)) != 0 for n in range(3)]
        out = []
        for s in range(2):
            rows = [jnp.broadcast_to(table[pl.ds(8 * s + c, 1), :], (16, 128)) for c in range(8)]
            rows = [jnp.concatenate([r] * (cls.shape[1] // 128), axis=1) for r in rows]
            rows = [jnp.where(bits[0], rows[2 * n + 1], rows[2 * n]) for n in range(4)]
            rows = [jnp.where(bits[1], rows[2 * n + 1], rows[2 * n]) for n in range(2)]
            out.append(jnp.where(bits[2], rows[1], rows[0]))
        return out

    def assemble_own(own, edge, size):
        def body(start):
            for j in range(size):
                x = start + j
                planes = [jnp.concatenate([own[x, f], edge[x, f]], axis=1) for f in range(3)]
                for s, d in enumerate(look_up(planes[2])):
                    b0[s, x + HX] = planes[s]
                    d0[s, x + HX] = d

        blocks(0, 16, size, body)

    def assemble_strip(strips, high, cut):
        second = (gx + high) % 2 == 1

        def plane(n):
            return jnp.where(second, strips[1][n], strips[0][n])

        lo = 20 * high
        for j in range(HX):
            for s, d in enumerate(look_up(plane(j))):
                d0[s, lo + j, :, cut] = d
        for s in range(2):
            for n in range(HX - 1):
                b0[s, lo + 1 - high + n, :, cut] = plane(HX + s * (HX - 1) + n)

    def masks(rows, step, factor, origin):
        lane = iota((rows, LN), 1)
        ypos = gy * 256 + jnp.where(lane < 256 + HY, lane, lane - LN)
        my = jnp.where((ypos >= step) & (ypos < ny), F32(factor), F32(0.0))
        mz = jnp.where(iota((rows, LN), 0) >= 1, F32(factor), F32(0.0))

        def factor_x(p):
            xpos = (gx * 16) // step + p - origin
            return jnp.where((xpos >= 1) & (xpos < nx // step), F32(factor), F32(0.0))

        return my, mz, factor_x

    def weigh(lo, hi, size, rows, step, factor, d, keep, v):
        blocks(lo, hi, size, weigher(size, rows, step, factor, d, keep, v))

    def weigher(size, rows, step, factor, d, keep, v):
        my, mz, factor_x = masks(rows, step, factor, HX if step == 1 else 6)

        def body(start):
            for s in range(2):
                face_weights(
                    d.at[s], keep[1].at[s], keep[2].at[s], keep[3].at[s], keep[4].at[s],
                    keep[0].at[s], v.at[s], start, size, factor_x, my, mz, step, 0 if step == 1 else 1,
                )

        return body

    def planes(keep, u, s, start, size, step):
        return stencil(
            u.at[s], keep[0].at[s], keep[1].at[s], keep[2].at[s], keep[3].at[s],
            start, size, step, 0 if step == 1 else 1,
        )

    def smooth(lo, hi, size, keep, v, step):
        blocks(lo, hi, size, smoother(size, keep, v, step))

    def smoother(size, keep, v, step):
        def body(start):
            for s in range(2):
                for p, here, r in planes(keep, v, s, start, size, step):
                    keep[5][s, p] = here + keep[4][s, p] * r

        return body

    def restrict(lo, hi, size):
        blocks(lo, hi, size, restricter(size))

    def restricter(size):
        def body(start):
            for s in range(2):
                res = [r for _, _, r in planes(keep0, u0, s, 2 * start - 8, 2 * size, 1)]
                for i in range(size):
                    total = res[2 * i] + res[2 * i + 1]
                    b1[s, start + i] = 0.125 * pair_lanes(total[:8] + total[8:], 1)

        return body

    def coarse_diff(lo, hi, size):
        def body(start):
            for i in range(size):
                for s in range(2):
                    p = 2 * (start + i) - 8
                    total = d0[s, p] + d0[s, p + 1]
                    d1[s, start + i] = 0.125 * pair_lanes(total[:8] + total[8:], 1)

        blocks(lo, hi, size, body)

    at = assemble_strip, weigher, smoother, restricter
    return assemble_own, at, weigh, smooth, restrict, coarse_diff, planes


FINE = 2.0 * STEP
COARSER = 0.5 * STEP


def own_kernel(table, own, edge, mfirst, msecond, *refs):
    keep0, keep1, (d0, v0, d1) = refs[:6], refs[6:12], refs[12:]
    assemble_own, at, weigh, smooth, restrict, coarse_diff, _ = fine_tools(
        table, keep0, keep1, d0, v0, d1
    )

    def one_side(high, carry):
        at[0]((mfirst, msecond), high, slice(0, 256))
        return carry

    lax.fori_loop(0, 2, one_side, 0)
    assemble_own(own, edge, 4)
    weigh(5, 19, 7, 16, 1, FINE, d0, keep0, v0)
    smooth(6, 18, 4, keep0, v0, 1)
    restrict(8, 12, 2)
    coarse_diff(6, 14, 4)


def near_kernel(
    table, sfirst, ssecond, *refs,
):
    first, second, *refs = refs[15:]
    keep0, keep1, (d0, v0, d1) = refs[:6], refs[6:12], refs[12:]
    _, at, _, _, _, _, _ = fine_tools(table, keep0, keep1, d0, v0, d1)
    assemble_strip, weigher, smoother, restricter = at
    weigh = weigher(4, 16, 1, FINE, d0, keep0, v0)
    smooth = smoother(4, keep0, v0, 1)
    restrict = restricter(2)

    def one_side(high, carry):
        assemble_strip((sfirst, ssecond), high, slice(256, LN))
        weigh(1 + 18 * high)
        smooth(2 + 16 * high)
        restrict(6 + 6 * high)
        return carry

    lax.fori_loop(0, 2, one_side, 0)
    odd = lax.axis_index("gx") % 2 == 1
    even_lane = iota((8, LN), 1) % 2 == 0

    def send(n, ref, low, high):
        low, high = (jnp.where(even_lane, ref[0, m], ref[1, m]) for m in (low, high))
        first[n] = jnp.where(odd, high, low)
        second[n] = jnp.where(odd, low, high)

    for k in range(4):
        send(k, keep1[0], 6 + k, 10 + k)
    for k in range(5):
        send(4 + k, d1, 6 + k, 9 + k)


def averaging(shape, dtype):
    group = iota(shape, 0) // 4
    target = jnp.where(group < (256 + HY) // 4, group + 16, group - 80)
    return jnp.where(iota(shape, 1) == target, F32(0.0625), F32(0.0)).astype(dtype)


def to_level2(rows, matrix, zs, message):
    rows = jnp.concatenate(rows, axis=0)
    high = rows.astype(BF16)
    rest = rows - high.astype(F32)
    middle = rest.astype(BF16)
    low = (rest - middle.astype(F32)).astype(BF16)
    whole = jnp.dot(
        jnp.concatenate([high, middle, low], axis=0), matrix, preferred_element_type=F32
    )
    whole = whole[0:64] + whole[64:128] + whole[128:192]
    lane = iota((8, 128), 1)
    halved = []
    for n in range(4):
        part = zs.at[n]
        part[...] = whole[16 * n : 16 * (n + 1)]
        halved.append(part[pl.ds(0, 8, stride=2), :] + part[pl.ds(1, 8, stride=2), :])
    for k in range(3):
        message[k] = jnp.where(lane < 96, halved[k], pltpu.roll(halved[3], 96 - 32 * k, 1))


def inner_kernel(d1, counts, *refs):
    keep1, (v1, react, diff2, matrix, zs) = refs[6:12], refs[12:]
    _, _, weigh, smooth, _, _, _ = fine_tools(None, keep1, keep1, None, None, d1)
    weigh(7, 13, 6, 8, 2, COARSER, d1, keep1, v1)
    smooth(8, 12, 4, keep1, v1, 2)
    for s in range(2):
        for x in range(16):
            halves = [counts[s, :, n, x, :] for n in range(2)]
            react[x, s] = REACT * (0.25 * jnp.concatenate(halves, axis=0).astype(F32))
    matrix[...] = averaging((LN, 128), BF16)
    rows = [d1[s, 6 + 2 * n] + d1[s, 7 + 2 * n] for n in range(4) for s in range(2)]
    to_level2(rows, matrix[...], zs, diff2)


def outer_kernel(first, second, diff2, matrix, *refs):
    message, *refs = refs[8:]
    keep1, (v1, d1, zs) = refs[:6], refs[6:]
    _, _, weigh, smooth, _, _, planes = fine_tools(None, keep1, keep1, None, None, d1)
    gx = lax.axis_index("gx")
    last = lax.axis_size("gx") - 1
    odd = gx % 2 == 1
    even_lane = iota((8, LN), 1) % 2 == 0

    def both(got, ref, m, real=None):
        if real is not None:
            got = jnp.where(real, got, F32(1.0))
        ref[0, m] = jnp.where(even_lane, got, shift_up(got, 1, 1))
        ref[1, m] = jnp.where(even_lane, shift_down(got, 1, 1), got)

    for k in range(9):
        low = jnp.where(odd, second[k], first[k])
        high = jnp.where(odd, first[k], second[k])
        if k < 4:
            both(low, keep1[0], 2 + k)
            both(high, keep1[0], 14 + k)
        else:
            both(low, d1, k - 3, gx > 0)
            both(high, d1, 10 + k, gx < last)
    for start in (2, 13):
        weigh(start, start + 5, 5, 8, 2, COARSER, d1, keep1, v1)
    for start in (3, 12):
        smooth(start, start + 5, 5, keep1, v1, 2)
    res = [[r for _, _, r in planes(keep1, keep1[5], s, 6, 8, 2)] for s in range(2)]
    rows = [res[s][2 * n] + res[s][2 * n + 1] for n in range(4) for s in range(2)]
    to_level2(rows, matrix[...], zs, message.at[0])
    message[1] = diff2[...]


def middle_kernel(gathered, tile, keep2, keep3, d2, d3, v2, v3, coarse):
    gy = lax.axis_index("gy")
    ny = 256 * lax.axis_size("gy")
    lane = iota((8, 128), 1)
    row = iota((8, 128), 0)
    ypos = gy * 64 + lane - 16
    zero = jnp.zeros((8, 128), F32)

    for keep, d, v, count in ((keep2, d2, v2, X2), (keep3, d3, v3, X3)):
        for k in range(PAD):
            for n in range(6):
                keep[n, k] = zero
                keep[n, count + PAD + k] = zero
        for p in (PAD - 1, PAD + count):
            d[p] = zero + 1.0
            v[p] = zero

    def level(keep, d, v, count, size, sy, sz, scale, nyl):
        factor = 2.0 * STEP * scale
        my = jnp.where((ypos >= sy) & (ypos < nyl), F32(factor), F32(0.0))
        mz = jnp.where(row % 4 >= sz, F32(factor), F32(0.0))

        def factor_x(p):
            return jnp.where((p > PAD) & (p < PAD + count), F32(factor), F32(0.0))

        def weights(start):
            face_weights(
                d, keep.at[1], keep.at[2], keep.at[3], keep.at[4], keep.at[0], v,
                start, size, factor_x, my, mz, sy, sz,
            )

        def planes(u, start, amount):
            return stencil(
                u, keep.at[0], keep.at[1], keep.at[2], keep.at[3], start, amount, sy, sz
            )

        def smooth(start):
            for p, here, r in planes(v, start, count):
                keep[5, p] = here + keep[4, p] * r

        blocks(PAD, PAD + count, size, weights)
        blocks(PAD, PAD + count, count, smooth)
        return planes

    for g in range(X2 // 4):
        for f, ref in ((0, keep2.at[0]), (1, d2)):
            packed = [gathered[g, f, k] for k in range(3)]
            fourth = [pltpu.roll(packed[k], 32 * (k + 1), 1) for k in range(3)]
            fourth = jnp.where(lane < 32, fourth[0], jnp.where(lane < 64, fourth[1], fourth[2]))
            for k, plane in enumerate(packed + [fourth]):
                ref[PAD + 4 * g + k] = plane
    planes2 = level(keep2, d2, v2, X2, X2, 1, 1, 0.0625, ny // 4)

    def restrict(start):
        first = 2 * (start - PAD) + PAD
        res = [r for _, _, r in planes2(keep2.at[5], first, X2)]
        for i in range(X3):
            total = res[2 * i] + res[2 * i + 1]
            keep3[0, start + i] = 0.125 * pair_rows(pair_lanes(total, 1), 1)
            total = d2[first + 2 * i] + d2[first + 2 * i + 1]
            d3[start + i] = 0.125 * pair_rows(pair_lanes(total, 1), 1)

    blocks(PAD, PAD + X3, X3, restrict)
    planes3 = level(keep3, d3, v3, X3, 32, 2, 2, 0.015625, ny // 4)

    def gather_pair(total):
        total = total + shift_down(total, 2, 1)
        return total + shift_down(total, 2, 0)

    res = [r for _, _, r in planes3(keep3.at[5], PAD, X3)]
    for i in range(X4):
        coarse[0, pl.ds(8 * i, 8), :] = gather_pair(res[2 * i] + res[2 * i + 1])
        coarse[1, pl.ds(8 * i, 8), :] = gather_pair(d3[PAD + 2 * i] + d3[PAD + 2 * i + 1])
    total = jnp.zeros((8, 128), F32)
    for g in range(8):
        f, s, half = g // 4, (g // 2) % 2, g % 2
        part = coarse[f, pl.ds(64 * half + 4 * s, 8, stride=8), :]
        part = pick_lanes(part, 16 + 4 * (lane % 16))
        total = jnp.where(lane // 16 == g, part, total)
    tile[...] = 0.125 * total


def coarsest(tiles):
    ngy = tiles.shape[0]
    width = 16 * ngy
    lane_group = iota((8, 128), 1) // 16
    fields = []
    for g in range(8):
        halves = []
        for h in range(width // 128):
            total = jnp.zeros((8, 128), F32)
            for q in range(8):
                piece = tiles[8 * h + q]
                shift = (16 * q - 16 * g) % 128
                if shift:
                    piece = pltpu.roll(piece, shift, 1)
                total = jnp.where(lane_group == q, piece, total)
            halves.append(total)
        fields.append(jnp.concatenate(halves, axis=1))
    whole = [jnp.concatenate([fields[2 * n], fields[2 * n + 1]], axis=0) for n in range(4)]
    shape = whole[0].shape
    factor = 2.0 * STEP * 0.25**4
    mx = jnp.where(iota(shape, 0) >= 1, F32(factor), F32(0.0))
    my = jnp.where(iota(shape, 1) >= 1, F32(factor), F32(0.0))
    out = []
    for s in range(2):
        b, d = whole[s], whole[2 + s]
        wx = mx * harm(d, shift_up(d, 1, 0))
        wy = my * harm(d, shift_up(d, 1, 1))
        inv = RELAX / (1.0 + (wx + shift_down(wx, 1, 0)) + (wy + shift_down(wy, 1, 1)))

        u = start = inv * b
        up_x, down_x = inv * wx, inv * shift_down(wx, 1, 0)
        up_y, down_y = inv * wy, inv * shift_down(wy, 1, 1)
        for _ in range(COARSE_SWEEPS - 1):
            along_x = up_x * shift_up(u, 1, 0) + down_x * shift_down(u, 1, 0)
            along_y = up_y * shift_up(u, 1, 1) + down_y * shift_down(u, 1, 1)
            u = ((1.0 - RELAX) * u + start) + (along_x + along_y)
        out.append(u + jnp.sum(b - u) / (shape[0] * shape[1]))
    return out


def up_kernel(
    tiles, keep2, keep3, react, *refs,
):
    keep0, keep1, (out, c4, rep2, u3, u2, p1, q1, q0) = refs[:6], refs[6:12], refs[12:]
    gx = lax.axis_index("gx")
    gy = lax.axis_index("gy")

    solved = jnp.concatenate(coarsest(tiles), axis=0)
    width = solved.shape[1]
    solved = pltpu.roll(solved, (width + 4 - 16 * gy) % width, 1)[:, :128]
    near = pick_lanes(solved, iota((1, 128), 1) // 4)
    for t in range(2):
        c4[t, pl.ds(0, 8), :] = jnp.zeros((8, 128), F32)
        c4[t, pl.ds(8, X4), :] = near[X4 * t : X4 * (t + 1)]
        c4[t, pl.ds(8 + X4, 8), :] = jnp.zeros((8, 128), F32)
    first_species = iota((8, 128), 0) < 4

    def coarse_plane(k):
        rows = [
            jnp.broadcast_to(c4[t, pl.ds(gx + 6 + k, 1), :], (8, 128)) for t in range(2)
        ]
        return jnp.where(first_species, rows[0], rows[1])

    def sweeps(keep, base, u, count, sy, sz):
        for turn in range(2):
            lo, hi = 1 + turn, count - 1 - turn
            here = u[lo]
            fx = keep[1, base + lo] * (here - u[lo - 1])
            for i in range(lo, hi):
                after = u[i + 1]
                fxn = keep[1, base + i + 1] * (after - here)
                r = residual_short(
                    here, keep[0, base + i], fx, fxn,
                    keep[2, base + i], keep[3, base + i], sy, sz,
                )
                u[i] = here + keep[4, base + i] * r
                here, fx = after, fxn

    base3 = gx * 2
    for i in range(0, 10, 2):
        plane = coarse_plane(i // 2)
        u3[i] = keep3[5, base3 + i] + plane
        u3[i + 1] = keep3[5, base3 + i + 1] + plane
    sweeps(keep3, base3, u3, 10, 2, 2)
    base2 = gx * 4
    for i in range(12):
        u2[i] = keep2[5, base2 + i] + u3[min(2 + i // 2, 9)]
    sweeps(keep2, base2, u2, 12, 1, 1)

    for i in range(8):
        for k in range(2):
            rep2[pl.ds(16 * i + k, 8, stride=2), :] = u2[2 + i]
    quarter = iota((1, 128), 1) // 4
    edge = jnp.where(quarter < 16, quarter + 80, quarter - 16)
    flat = [pick_lanes(rep2[...], lanes) for lanes in (quarter + 16, quarter + 48, edge)]
    c2 = jnp.concatenate(flat, axis=1).reshape(8, 2, 8, LN)

    def planes(keep, u, s, start, size, step):
        return stencil(
            u.at[s], keep[0].at[s], keep[1].at[s], keep[2].at[s], keep[3].at[s],
            start, size, step, 0 if step == 1 else 1,
        )

    def smooth(lo, hi, size, keep, u, new, step):
        def body(start):
            for s in range(2):
                for p, here, r in planes(keep, u, s, start, size, step):
                    new[s, p] = here + keep[4][s, p] * r

        blocks(lo, hi, size, body)

    for i in range(3, 17):
        for s in range(2):
            p1[s, i] = keep1[5][s, i] + c2[(i - 6) // 2 + 2, s]
    smooth(4, 16, 12, keep1, p1, q1, 2)
    smooth(5, 15, 10, keep1, q1, p1, 2)

    def corrected_sweep(n, carry):
        start = 3 + 6 * n
        for s in range(2):
            spread = [p1[s, 5 + 3 * n + j] for j in range(4)]
            spread = [jnp.concatenate([c, c], axis=0) for c in spread]
            u = [keep0[5][s, start - 1 + j] + spread[j // 2] for j in range(8)]
            fx = keep0[1][s, start] * (u[1] - u[0])
            for j in range(6):
                p = start + j
                fxn = keep0[1][s, p + 1] * (u[j + 2] - u[j + 1])
                r = residual(
                    u[j + 1], keep0[0][s, p], fx, fxn, keep0[2][s, p], keep0[3][s, p], 1, 0
                )
                q0[s, p] = u[j + 1] + keep0[4][s, p] * r
                fx = fxn
        return carry

    lax.fori_loop(0, 3, corrected_sweep, 0)

    def last(start):
        adj = [[], []]
        for s in range(2):
            for p, here, r in planes(keep0, q0, s, start, 4, 1):
                adj[s].append((here + keep0[4][s, p] * r)[:, :256])
        for j in range(4):
            x = start + j - HX
            a0, a1 = adj[0][j], adj[1][j]
            total = a0 + a1
            for s, value in enumerate((a0 - react[x, 1] * total, a1 - react[x, 0] * total)):
                out[s, :, 0, x, :] = value[:8]
                out[s, :, 1, x, :] = value[8:]

    blocks(4, 20, 4, last)


def call(
    kernel, outs, scratch, args, name, limit, kinds=None, aliases=None, cycles=0, dtypes=None
):
    spaces = {"v": pltpu.VMEM, "s": pltpu.SMEM}
    specs = [pl.BlockSpec(memory_space=spaces[k]) for k in kinds or "v" * len(args)]
    return pl.pallas_call(
        kernel,
        out_shape=[jax.ShapeDtypeStruct(o, d) for o, d in zip(outs, dtypes or [F32] * len(outs))],
        in_specs=specs,
        out_specs=[pl.BlockSpec(memory_space=pltpu.VMEM)] * len(outs),
        scratch_shapes=[pltpu.VMEM(s, F32) if isinstance(s, tuple) else s for s in scratch],
        input_output_aliases=aliases or {},
        compiler_params=pltpu.CompilerParams(vmem_limit_bytes=limit * 1024 * 1024),
        cost_estimate=pl.CostEstimate(flops=cycles, bytes_accessed=0, transcendentals=0)
        if cycles
        else None,
        name=name,
    )(*args)


def swap(axis, first, block):
    pairs = [(i, i + 1) for i in range(first, lax.axis_size(axis) - 1, 2)]
    return lax.ppermute(block, axis, pairs + [(j, i) for i, j in pairs])


def everyone(block, axis):
    count = lax.axis_size(axis)
    copies = jnp.broadcast_to(block[None], (count,) + block.shape)
    return lax.all_to_all(copies, axis, split_axis=0, concat_axis=0, tiled=True)


def per_device(counts, classes, diffusivity, cotangent):
    shape = cotangent.shape
    counts, cotangent = (a.reshape(2, 8, 2, 16, 256) for a in (counts, cotangent))
    classes = classes.reshape(8, 2, 16, 256)
    (start,) = call(first_kernel, [(8, 128)], [], (), "first", 8, cycles=10**9)
    (table,) = call(table_kernel, [(16, 128)], [], (diffusivity,), "table", 8)
    own, across, inside = call(
        turn_kernel,
        [(16, 3, 16, 256), (8, 3, 16, 128), (8, 3, 16, 128)], [],
        (cotangent, classes, start), "turn", 8,
    )
    across, inside = swap("gy", 1, across), swap("gy", 0, inside)
    strip = (3 * HX - 2, 16, 256)
    mfirst, msecond = call(cut_strips, [strip, strip], [], (own,), "strips", 8)
    mfirst, msecond = swap("gx", 1, mfirst), swap("gx", 0, msecond)
    strip = (3 * HX - 2, 16, 128)
    edge, sfirst, ssecond = call(
        edge_kernel, [(16, 3, 16, 128), strip, strip], [], (across, inside), "edge", 8
    )
    sfirst, ssecond = swap("gx", 1, sfirst), swap("gx", 0, ssecond)
    level0, level1 = (2, NPL, 16, LN), (2, N1, 8, LN)
    fine = [level0] * 6 + [level1] * 6 + [level0] * 2 + [level1]
    kept = call(own_kernel, fine, [], (table, own, edge, mfirst, msecond), "own", 8, cycles=10**7)
    strip = (9, 8, LN)
    first, second, *kept = call(
        near_kernel,
        [strip, strip] + fine, [],
        (table, sfirst, ssecond, *kept), "near", 8,
        aliases={3 + n: 2 + n for n in range(15)},
    )
    keep0, keep1, d1 = kept[:6], kept[6:12], kept[14]
    first, second = swap("gx", 1, first), swap("gx", 0, second)
    zs = (4, 16, 128)
    *keep1, v1, react, diff2, matrix = call(
        inner_kernel, [level1] * 7 + [(16, 2, 16, 256), (3, 8, 128), (LN, 128)], [zs],
        (d1, counts, *keep1), "inner", 8,
        aliases={2 + n: n for n in range(6)}, cycles=10**7, dtypes=[F32] * 9 + [BF16],
    )
    message, *keep1, _, _ = call(
        outer_kernel, [(2, 3, 8, 128)] + [level1] * 8, [zs],
        (first, second, diff2, matrix, *keep1, v1, d1), "outer", 8,
        aliases={4 + n: 1 + n for n in range(8)},
    )
    gathered = everyone(message, "gx")
    tile, keep2, keep3 = call(
        middle_kernel,
        [(8, 128), (6, X2 + 2 * PAD, 8, 128), (6, X3 + 2 * PAD, 8, 128)],
        [(X2 + 2 * PAD, 8, 128), (X3 + 2 * PAD, 8, 128)] * 2 + [(2, 128, 128)],
        (gathered,), "middle", 8,
    )
    tiles = everyone(tile, "gy")
    (gradient,) = call(
        up_kernel,
        [(2, 8, 2, 16, 256)],
        [
            (2, X4 + 16, 128), (128, 128), (10, 8, 128), (12, 8, 128),
            (2, N1, 8, LN), (2, N1, 8, LN), (2, NPL, 16, LN),
        ],
        (tiles, keep2, keep3, react, *keep0, *keep1), "up", 12,
    )
    return gradient.reshape(shape)


def solution(mesh):
    in_specs = (P(None, None, "gx", "gy"), P(None, "gx", "gy"), P(), P(None, None, "gx", "gy"))
    out_specs = P(None, None, "gx", "gy")
    return jax.shard_map(
        per_device, mesh=mesh, in_specs=in_specs, out_specs=out_specs, check_vma=False
    )
```

```python
import jax
import jax.numpy as jnp
from jax import lax
from jax.experimental import pallas as pl
from jax.experimental.pallas import tpu as pltpu
from jax.sharding import PartitionSpec as P

F32 = jnp.float32
BF16 = jnp.bfloat16
RELAX = 0.8
REACT = 0.3
STEP = 256.0
COARSE_SWEEPS = 8

HX = 4
NPL = 16 + 2 * HX
N1 = 20
HY = 64
LN = 384
PAD = 4
X2 = 64
X3 = 32
X4 = 16


def iota(shape, axis):
    return lax.broadcasted_iota(jnp.int32, shape, axis)


def shift_up(value, by, axis):
    return pltpu.roll(value, by, axis)


def shift_down(value, by, axis):
    return pltpu.roll(value, value.shape[axis] - by, axis)


def reciprocal(x):
    return pl.reciprocal(x, approx=True)


def z_up(value, step):
    if step:
        return shift_up(value, step, 0)
    return jnp.concatenate([shift_up(value[8:], 1, 0), value[:8]], axis=0)


def z_down(value, step):
    if step:
        return shift_down(value, step, 0)
    return jnp.concatenate([value[8:], shift_down(value[:8], 1, 0)], axis=0)


def harm(a, b):
    return a * b * reciprocal(a + b)


def residual(u, b, fx, fxn, wy, wz, sy, sz):
    fy = wy * (u - shift_up(u, sy, 1))
    mu = u + (fx - fxn) + (fy - shift_down(fy, sy, 1))
    fz = wz * (u - z_up(u, sz))
    return b - (mu + (fz - z_down(fz, sz)))


def residual_short(u, b, fx, fxn, wy, wz, sy, sz):
    fy = wy * (u - shift_up(u, sy, 1)) - shift_down(wy, sy, 1) * (shift_down(u, sy, 1) - u)
    fz = wz * (u - z_up(u, sz)) - z_down(wz, sz) * (z_down(u, sz) - u)
    return b - (u + (fx - fxn) + (fy + fz))


def diagonal(wx, wxn, wy, wz, sy, sz):
    return 1.0 + (wx + wxn) + (wy + shift_down(wy, sy, 1)) + (wz + z_down(wz, sz))


def pair_lanes(value, half):
    width = value.shape[1]
    total = value + shift_down(value, half, 1)
    first = (iota(value.shape, 1) // half) % 2 == 0
    return jnp.where(first, total, shift_up(total, half, 1))


def pair_rows(value, half):
    total = value + shift_down(value, half, 0)
    first = (iota(value.shape, 0) // half) % 2 == 0
    return jnp.where(first, total, shift_up(total, half, 0))


def pick_lanes(value, lanes):
    return jnp.take_along_axis(value, jnp.broadcast_to(lanes, value.shape), axis=1)


def stencil(u, b, wx, wy, wz, start, count, sy, sz):
    here = u[start]
    fx = wx[start] * (here - u[start - 1])
    for j in range(count):
        p = start + j
        after = u[p + 1]
        fxn = wx[p + 1] * (after - here)
        yield p, here, residual(here, b[p], fx, fxn, wy[p], wz[p], sy, sz)
        here, fx = after, fxn


def pair_sums(residuals):
    sums, first = [], None
    for _, _, r in residuals:
        if first is None:
            first = r
        else:
            sums.append(first + r)
            first = None
    return sums


def face_weights(d, wx, wy, wz, inv, b, u, start, count, factor_x, my, mz, sy, sz):
    here = d[start]
    side = factor_x(start) * harm(here, d[start - 1])
    for j in range(count):
        p = start + j
        after = d[p + 1]
        siden = factor_x(p + 1) * harm(after, here)
        y = my * harm(here, shift_up(here, sy, 1))
        z = mz * harm(here, z_up(here, sz))
        wx[p], wy[p], wz[p] = side, y, z
        value = RELAX * reciprocal(diagonal(side, siden, y, z, sy, sz))
        inv[p] = value
        u[p] = value * b[p]
        here, side = after, siden


def blocks(lo, hi, size, body):
    assert (hi - lo) % size == 0
    if hi - lo == size:
        body(lo)
        return

    def step(n, carry):
        body(lo + n * size)
        return carry

    lax.fori_loop(0, (hi - lo) // size, step, 0)


def table_kernel(diff_ref, table):
    for s in range(2):
        for c in range(8):
            value = diff_ref[pl.ds(s, 1), pl.ds(c, 1)]
            table[pl.ds(8 * s + c, 1), :] = jnp.broadcast_to(value, (1, 128))


def first_kernel(out):
    out[...] = jnp.zeros((8, 128), F32)


def turn_kernel(cot, cls, start, own, across, inside):
    odd = lax.axis_index("gy") % 2 == 1
    left_half = iota((16, 128), 1) < HY
    for f in range(3):
        for k in range(8):
            pair = []
            for x in (k, k + 8):
                halves = [cls[:, n, x, :] if f == 2 else cot[f, :, n, x, :] for n in range(2)]
                pair.append(jnp.concatenate(halves, axis=0).astype(F32))
                own[x, f] = pair[-1]
            a, b = pair
            to_left = jnp.where(left_half, a[:, :128], pltpu.roll(b[:, :128], HY, 1))
            to_right = jnp.where(left_half, pltpu.roll(b[:, 128:], HY, 1), a[:, 128:])
            across[k, f] = jnp.where(odd, to_right, to_left)
            inside[k, f] = jnp.where(odd, to_left, to_right)


def cut_strips(planes, first, second):
    odd = lax.axis_index("gx") % 2 == 1
    for f in range(3):
        place = 0 if f == 2 else HX + f * (HX - 1)
        count = HX if f == 2 else HX - 1
        for n in range(count):
            low, high = planes[n, f], planes[16 - count + n, f]
            first[place + n] = jnp.where(odd, high, low)
            second[place + n] = jnp.where(odd, low, high)


def edge_kernel(across, inside, edge, first, second):
    odd = lax.axis_index("gy") % 2 == 1
    left_half = iota((16, 128), 1) < HY
    for k in range(8):
        for f in range(3):
            got = across[k, f], inside[k, f]
            fl, fr = jnp.where(odd, got[1], got[0]), jnp.where(odd, got[0], got[1])
            edge[k, f] = jnp.where(left_half, fr, fl)
            edge[k + 8, f] = pltpu.roll(jnp.where(left_half, fl, fr), HY, 1)
    cut_strips(edge, first, second)


def fine_tools(table, keep0, keep1, d0, v0, d1):
    gx = lax.axis_index("gx")
    gy = lax.axis_index("gy")
    nx = 16 * lax.axis_size("gx")
    ny = 256 * lax.axis_size("gy")
    b0, u0, b1 = keep0[0], keep0[5], keep1[0]

    def look_up(values):
        cls = values.astype(jnp.int32)
        bits = [(cls & (1 << n)) != 0 for n in range(3)]
        out = []
        for s in range(2):
            rows = [jnp.broadcast_to(table[pl.ds(8 * s + c, 1), :], (16, 128)) for c in range(8)]
            rows = [jnp.concatenate([r] * (cls.shape[1] // 128), axis=1) for r in rows]
            rows = [jnp.where(bits[0], rows[2 * n + 1], rows[2 * n]) for n in range(4)]
            rows = [jnp.where(bits[1], rows[2 * n + 1], rows[2 * n]) for n in range(2)]
            out.append(jnp.where(bits[2], rows[1], rows[0]))
        return out

    def assemble_own(own, edge, size):
        def body(start):
            for j in range(size):
                x = start + j
                planes = [jnp.concatenate([own[x, f], edge[x, f]], axis=1) for f in range(3)]
                for s, d in enumerate(look_up(planes[2])):
                    b0[s, x + HX] = planes[s]
                    d0[s, x + HX] = d

        blocks(0, 16, size, body)

    def assemble_strip(strips, high, cut):
        second = (gx + high) % 2 == 1

        def plane(n):
            return jnp.where(second, strips[1][n], strips[0][n])

        lo = 20 * high
        for j in range(HX):
            for s, d in enumerate(look_up(plane(j))):
                d0[s, lo + j, :, cut] = d
        for s in range(2):
            for n in range(HX - 1):
                b0[s, lo + 1 - high + n, :, cut] = plane(HX + s * (HX - 1) + n)

    def masks(rows, step, factor, origin):
        lane = iota((rows, LN), 1)
        ypos = gy * 256 + jnp.where(lane < 256 + HY, lane, lane - LN)
        my = jnp.where((ypos >= step) & (ypos < ny), F32(factor), F32(0.0))
        mz = jnp.where(iota((rows, LN), 0) >= 1, F32(factor), F32(0.0))

        def factor_x(p):
            xpos = (gx * 16) // step + p - origin
            return jnp.where((xpos >= 1) & (xpos < nx // step), F32(factor), F32(0.0))

        return my, mz, factor_x

    def weigh(lo, hi, size, rows, step, factor, d, keep, v):
        blocks(lo, hi, size, weigher(size, rows, step, factor, d, keep, v))

    def weigher(size, rows, step, factor, d, keep, v):
        my, mz, factor_x = masks(rows, step, factor, HX if step == 1 else 6)

        def body(start):
            for s in range(2):
                face_weights(
                    d.at[s], keep[1].at[s], keep[2].at[s], keep[3].at[s], keep[4].at[s],
                    keep[0].at[s], v.at[s], start, size, factor_x, my, mz, step, 0 if step == 1 else 1,
                )

        return body

    def planes(keep, u, s, start, size, step):
        return stencil(
            u.at[s], keep[0].at[s], keep[1].at[s], keep[2].at[s], keep[3].at[s],
            start, size, step, 0 if step == 1 else 1,
        )

    def smooth(lo, hi, size, keep, v, step):
        blocks(lo, hi, size, smoother(size, keep, v, step))

    def smoother(size, keep, v, step):
        def body(start):
            for s in range(2):
                for p, here, r in planes(keep, v, s, start, size, step):
                    keep[5][s, p] = here + keep[4][s, p] * r

        return body

    def restrict(lo, hi, size):
        blocks(lo, hi, size, restricter(size))

    def restricter(size):
        def body(start):
            for s in range(2):
                res = [r for _, _, r in planes(keep0, u0, s, 2 * start - 8, 2 * size, 1)]
                for i in range(size):
                    total = res[2 * i] + res[2 * i + 1]
                    b1[s, start + i] = 0.125 * pair_lanes(total[:8] + total[8:], 1)

        return body

    def coarse_diff(lo, hi, size):
        def body(start):
            for i in range(size):
                for s in range(2):
                    p = 2 * (start + i) - 8
                    total = d0[s, p] + d0[s, p + 1]
                    d1[s, start + i] = 0.125 * pair_lanes(total[:8] + total[8:], 1)

        blocks(lo, hi, size, body)

    at = assemble_strip, weigher, smoother, restricter
    return assemble_own, at, weigh, smooth, restrict, coarse_diff, planes


FINE = 2.0 * STEP
COARSER = 0.5 * STEP


def own_kernel(table, own, edge, mfirst, msecond, *refs):
    keep0, keep1, (d0, v0, d1) = refs[:6], refs[6:12], refs[12:]
    assemble_own, at, weigh, smooth, restrict, coarse_diff, _ = fine_tools(
        table, keep0, keep1, d0, v0, d1
    )

    def one_side(high, carry):
        at[0]((mfirst, msecond), high, slice(0, 256))
        return carry

    lax.fori_loop(0, 2, one_side, 0)
    assemble_own(own, edge, 4)
    weigh(5, 19, 7, 16, 1, FINE, d0, keep0, v0)
    smooth(6, 18, 4, keep0, v0, 1)
    restrict(8, 12, 2)
    coarse_diff(6, 14, 4)


def near_kernel(
    table, sfirst, ssecond, *refs,
):
    first, second, *refs = refs[15:]
    keep0, keep1, (d0, v0, d1) = refs[:6], refs[6:12], refs[12:]
    _, at, _, _, _, _, _ = fine_tools(table, keep0, keep1, d0, v0, d1)
    assemble_strip, weigher, smoother, restricter = at
    weigh = weigher(4, 16, 1, FINE, d0, keep0, v0)
    smooth = smoother(4, keep0, v0, 1)
    restrict = restricter(2)

    def one_side(high, carry):
        assemble_strip((sfirst, ssecond), high, slice(256, LN))
        weigh(1 + 18 * high)
        smooth(2 + 16 * high)
        restrict(6 + 6 * high)
        return carry

    lax.fori_loop(0, 2, one_side, 0)
    odd = lax.axis_index("gx") % 2 == 1
    even_lane = iota((8, LN), 1) % 2 == 0

    def send(n, ref, low, high):
        low, high = (jnp.where(even_lane, ref[0, m], ref[1, m]) for m in (low, high))
        first[n] = jnp.where(odd, high, low)
        second[n] = jnp.where(odd, low, high)

    for k in range(4):
        send(k, keep1[0], 6 + k, 10 + k)
    for k in range(5):
        send(4 + k, d1, 6 + k, 9 + k)


def averaging(shape, dtype):
    group = iota(shape, 0) // 4
    target = jnp.where(group < (256 + HY) // 4, group + 16, group - 80)
    return jnp.where(iota(shape, 1) == target, F32(0.0625), F32(0.0)).astype(dtype)


def to_level2(rows, matrix, zs, message):
    rows = jnp.concatenate(rows, axis=0)
    high = rows.astype(BF16)
    rest = rows - high.astype(F32)
    middle = rest.astype(BF16)
    low = (rest - middle.astype(F32)).astype(BF16)
    whole = jnp.dot(
        jnp.concatenate([high, middle, low], axis=0), matrix, preferred_element_type=F32
    )
    whole = whole[0:64] + whole[64:128] + whole[128:192]
    lane = iota((8, 128), 1)
    halved = []
    for n in range(4):
        part = zs.at[n]
        part[...] = whole[16 * n : 16 * (n + 1)]
        halved.append(part[pl.ds(0, 8, stride=2), :] + part[pl.ds(1, 8, stride=2), :])
    for k in range(3):
        message[k] = jnp.where(lane < 96, halved[k], pltpu.roll(halved[3], 96 - 32 * k, 1))


def inner_kernel(d1, counts, *refs):
    keep1, (v1, react, diff2, matrix, zs) = refs[6:12], refs[12:]
    _, _, weigh, smooth, _, _, _ = fine_tools(None, keep1, keep1, None, None, d1)
    weigh(7, 13, 6, 8, 2, COARSER, d1, keep1, v1)
    smooth(8, 12, 4, keep1, v1, 2)
    for s in range(2):
        for x in range(16):
            halves = [counts[s, :, n, x, :] for n in range(2)]
            react[x, s] = REACT * (0.25 * jnp.concatenate(halves, axis=0).astype(F32))
    matrix[...] = averaging((LN, 128), BF16)
    rows = [d1[s, 6 + 2 * n] + d1[s, 7 + 2 * n] for n in range(4) for s in range(2)]
    to_level2(rows, matrix[...], zs, diff2)


def outer_kernel(first, second, diff2, matrix, *refs):
    message, *refs = refs[8:]
    keep1, (v1, d1, zs) = refs[:6], refs[6:]
    _, _, weigh, smooth, _, _, planes = fine_tools(None, keep1, keep1, None, None, d1)
    gx = lax.axis_index("gx")
    last = lax.axis_size("gx") - 1
    odd = gx % 2 == 1
    even_lane = iota((8, LN), 1) % 2 == 0

    def both(got, ref, m, real=None):
        if real is not None:
            got = jnp.where(real, got, F32(1.0))
        ref[0, m] = jnp.where(even_lane, got, shift_up(got, 1, 1))
        ref[1, m] = jnp.where(even_lane, shift_down(got, 1, 1), got)

    for k in range(9):
        low = jnp.where(odd, second[k], first[k])
        high = jnp.where(odd, first[k], second[k])
        if k < 4:
            both(low, keep1[0], 2 + k)
            both(high, keep1[0], 14 + k)
        else:
            both(low, d1, k - 3, gx > 0)
            both(high, d1, 10 + k, gx < last)
    for start in (2, 13):
        weigh(start, start + 5, 5, 8, 2, COARSER, d1, keep1, v1)
    for start in (3, 12):
        smooth(start, start + 5, 5, keep1, v1, 2)
    res = [pair_sums(planes(keep1, keep1[5], s, 6, 8, 2)) for s in range(2)]
    rows = [res[s][n] for n in range(4) for s in range(2)]
    to_level2(rows, matrix[...], zs, message.at[0])
    message[1] = diff2[...]


def middle_kernel(gathered, tile, keep2, keep3, d2, d3, v2, v3, coarse):
    gy = lax.axis_index("gy")
    ny = 256 * lax.axis_size("gy")
    lane = iota((8, 128), 1)
    row = iota((8, 128), 0)
    ypos = gy * 64 + lane - 16
    zero = jnp.zeros((8, 128), F32)

    for keep, d, v, count in ((keep2, d2, v2, X2), (keep3, d3, v3, X3)):
        for k in range(PAD):
            for n in range(6):
                keep[n, k] = zero
                keep[n, count + PAD + k] = zero
        for p in (PAD - 1, PAD + count):
            d[p] = zero + 1.0
            v[p] = zero

    def level(keep, d, v, count, size, sy, sz, scale, nyl):
        factor = 2.0 * STEP * scale
        my = jnp.where((ypos >= sy) & (ypos < nyl), F32(factor), F32(0.0))
        mz = jnp.where(row % 4 >= sz, F32(factor), F32(0.0))

        def factor_x(p):
            return jnp.where((p > PAD) & (p < PAD + count), F32(factor), F32(0.0))

        def weights(start):
            face_weights(
                d, keep.at[1], keep.at[2], keep.at[3], keep.at[4], keep.at[0], v,
                start, size, factor_x, my, mz, sy, sz,
            )

        def planes(u, start, amount):
            return stencil(
                u, keep.at[0], keep.at[1], keep.at[2], keep.at[3], start, amount, sy, sz
            )

        def smooth(start):
            for p, here, r in planes(v, start, count):
                keep[5, p] = here + keep[4, p] * r

        blocks(PAD, PAD + count, size, weights)
        blocks(PAD, PAD + count, count, smooth)
        return planes

    for g in range(X2 // 4):
        for f, ref in ((0, keep2.at[0]), (1, d2)):
            packed = [gathered[g, f, k] for k in range(3)]
            fourth = [pltpu.roll(packed[k], 32 * (k + 1), 1) for k in range(3)]
            fourth = jnp.where(lane < 32, fourth[0], jnp.where(lane < 64, fourth[1], fourth[2]))
            for k, plane in enumerate(packed + [fourth]):
                ref[PAD + 4 * g + k] = plane
    planes2 = level(keep2, d2, v2, X2, X2, 1, 1, 0.0625, ny // 4)

    def restrict(start):
        first = 2 * (start - PAD) + PAD
        res = pair_sums(planes2(keep2.at[5], first, X2))
        for i in range(X3):
            total = res[i]
            keep3[0, start + i] = 0.125 * pair_rows(pair_lanes(total, 1), 1)
            total = d2[first + 2 * i] + d2[first + 2 * i + 1]
            d3[start + i] = 0.125 * pair_rows(pair_lanes(total, 1), 1)

    blocks(PAD, PAD + X3, X3, restrict)
    planes3 = level(keep3, d3, v3, X3, 32, 2, 2, 0.015625, ny // 4)

    def gather_pair(total):
        total = total + shift_down(total, 2, 1)
        return total + shift_down(total, 2, 0)

    res = pair_sums(planes3(keep3.at[5], PAD, X3))
    for i in range(X4):
        coarse[0, pl.ds(8 * i, 8), :] = gather_pair(res[i])
        coarse[1, pl.ds(8 * i, 8), :] = gather_pair(d3[PAD + 2 * i] + d3[PAD + 2 * i + 1])
    total = jnp.zeros((8, 128), F32)
    for g in range(8):
        f, s, half = g // 4, (g // 2) % 2, g % 2
        part = coarse[f, pl.ds(64 * half + 4 * s, 8, stride=8), :]
        part = pick_lanes(part, 16 + 4 * (lane % 16))
        total = jnp.where(lane // 16 == g, part, total)
    tile[...] = 0.125 * total


def coarsest(tiles):
    ngy = tiles.shape[0]
    width = 16 * ngy
    lane_group = iota((8, 128), 1) // 16
    fields = []
    for g in range(8):
        halves = []
        for h in range(width // 128):
            total = jnp.zeros((8, 128), F32)
            for q in range(8):
                piece = tiles[8 * h + q]
                shift = (16 * q - 16 * g) % 128
                if shift:
                    piece = pltpu.roll(piece, shift, 1)
                total = jnp.where(lane_group == q, piece, total)
            halves.append(total)
        fields.append(jnp.concatenate(halves, axis=1))
    whole = [jnp.concatenate([fields[2 * n], fields[2 * n + 1]], axis=0) for n in range(4)]
    shape = whole[0].shape
    factor = 2.0 * STEP * 0.25**4
    mx = jnp.where(iota(shape, 0) >= 1, F32(factor), F32(0.0))
    my = jnp.where(iota(shape, 1) >= 1, F32(factor), F32(0.0))
    out = []
    for s in range(2):
        b, d = whole[s], whole[2 + s]
        wx = mx * harm(d, shift_up(d, 1, 0))
        wy = my * harm(d, shift_up(d, 1, 1))
        inv = RELAX / (1.0 + (wx + shift_down(wx, 1, 0)) + (wy + shift_down(wy, 1, 1)))

        u = start = inv * b
        up_x, down_x = inv * wx, inv * shift_down(wx, 1, 0)
        up_y, down_y = inv * wy, inv * shift_down(wy, 1, 1)
        for _ in range(COARSE_SWEEPS - 1):
            along_x = up_x * shift_up(u, 1, 0) + down_x * shift_down(u, 1, 0)
            along_y = up_y * shift_up(u, 1, 1) + down_y * shift_down(u, 1, 1)
            u = ((1.0 - RELAX) * u + start) + (along_x + along_y)
        out.append(u + jnp.sum(b - u) / (shape[0] * shape[1]))
    return out


def up_kernel(
    tiles, keep2, keep3, react, *refs,
):
    keep0, keep1, (out, c4, rep2, u3, u2, p1, q1, q0) = refs[:6], refs[6:12], refs[12:]
    gx = lax.axis_index("gx")
    gy = lax.axis_index("gy")

    solved = jnp.concatenate(coarsest(tiles), axis=0)
    width = solved.shape[1]
    solved = pltpu.roll(solved, (width + 4 - 16 * gy) % width, 1)[:, :128]
    near = pick_lanes(solved, iota((1, 128), 1) // 4)
    for t in range(2):
        c4[t, pl.ds(0, 8), :] = jnp.zeros((8, 128), F32)
        c4[t, pl.ds(8, X4), :] = near[X4 * t : X4 * (t + 1)]
        c4[t, pl.ds(8 + X4, 8), :] = jnp.zeros((8, 128), F32)
    first_species = iota((8, 128), 0) < 4

    def coarse_plane(k):
        rows = [
            jnp.broadcast_to(c4[t, pl.ds(gx + 6 + k, 1), :], (8, 128)) for t in range(2)
        ]
        return jnp.where(first_species, rows[0], rows[1])

    def sweeps(keep, base, u, count, sy, sz):
        for turn in range(2):
            lo, hi = 1 + turn, count - 1 - turn
            here = u[lo]
            fx = keep[1, base + lo] * (here - u[lo - 1])
            for i in range(lo, hi):
                after = u[i + 1]
                fxn = keep[1, base + i + 1] * (after - here)
                r = residual_short(
                    here, keep[0, base + i], fx, fxn,
                    keep[2, base + i], keep[3, base + i], sy, sz,
                )
                u[i] = here + keep[4, base + i] * r
                here, fx = after, fxn

    base3 = gx * 2
    for i in range(0, 10, 2):
        plane = coarse_plane(i // 2)
        u3[i] = keep3[5, base3 + i] + plane
        u3[i + 1] = keep3[5, base3 + i + 1] + plane
    sweeps(keep3, base3, u3, 10, 2, 2)
    base2 = gx * 4
    for i in range(12):
        u2[i] = keep2[5, base2 + i] + u3[min(2 + i // 2, 9)]
    sweeps(keep2, base2, u2, 12, 1, 1)

    for i in range(8):
        for k in range(2):
            rep2[pl.ds(16 * i + k, 8, stride=2), :] = u2[2 + i]
    quarter = iota((1, 128), 1) // 4
    edge = jnp.where(quarter < 16, quarter + 80, quarter - 16)
    flat = [pick_lanes(rep2[...], lanes) for lanes in (quarter + 16, quarter + 48, edge)]
    c2 = jnp.concatenate(flat, axis=1).reshape(8, 2, 8, LN)

    def planes(keep, u, s, start, size, step):
        return stencil(
            u.at[s], keep[0].at[s], keep[1].at[s], keep[2].at[s], keep[3].at[s],
            start, size, step, 0 if step == 1 else 1,
        )

    def smooth(lo, hi, size, keep, u, new, step):
        def body(start):
            for s in range(2):
                for p, here, r in planes(keep, u, s, start, size, step):
                    new[s, p] = here + keep[4][s, p] * r

        blocks(lo, hi, size, body)

    for i in range(3, 17):
        for s in range(2):
            p1[s, i] = keep1[5][s, i] + c2[(i - 6) // 2 + 2, s]
    smooth(4, 16, 12, keep1, p1, q1, 2)
    smooth(5, 15, 10, keep1, q1, p1, 2)

    def corrected_sweep(n, carry):
        start = 3 + 6 * n
        for s in range(2):
            spread = [p1[s, 5 + 3 * n + j] for j in range(4)]
            spread = [jnp.concatenate([c, c], axis=0) for c in spread]

            def corrected(j):
                return keep0[5][s, start - 1 + j] + spread[j // 2]

            here = corrected(1)
            fx = keep0[1][s, start] * (here - corrected(0))
            for j in range(6):
                p = start + j
                after = corrected(j + 2)
                fxn = keep0[1][s, p + 1] * (after - here)
                r = residual(here, keep0[0][s, p], fx, fxn, keep0[2][s, p], keep0[3][s, p], 1, 0)
                q0[s, p] = here + keep0[4][s, p] * r
                here = after
                fx = fxn
        return carry

    lax.fori_loop(0, 3, corrected_sweep, 0)

    def last(start):
        for pair in zip(*(planes(keep0, q0, s, start, 8, 1) for s in range(2))):
            p = pair[0][0]
            a0, a1 = (
                (here + keep0[4][s, p] * r)[:, :256] for s, (_, here, r) in enumerate(pair)
            )
            x = p - HX
            total = a0 + a1
            for s, value in enumerate((a0 - react[x, 1] * total, a1 - react[x, 0] * total)):
                out[s, :, 0, x, :] = value[:8]
                out[s, :, 1, x, :] = value[8:]

    blocks(4, 20, 8, last)


def call(
    kernel, outs, scratch, args, name, limit, kinds=None, aliases=None, cycles=0, dtypes=None
):
    spaces = {"v": pltpu.VMEM, "s": pltpu.SMEM}
    specs = [pl.BlockSpec(memory_space=spaces[k]) for k in kinds or "v" * len(args)]
    return pl.pallas_call(
        kernel,
        out_shape=[jax.ShapeDtypeStruct(o, d) for o, d in zip(outs, dtypes or [F32] * len(outs))],
        in_specs=specs,
        out_specs=[pl.BlockSpec(memory_space=pltpu.VMEM)] * len(outs),
        scratch_shapes=[pltpu.VMEM(s, F32) if isinstance(s, tuple) else s for s in scratch],
        input_output_aliases=aliases or {},
        compiler_params=pltpu.CompilerParams(vmem_limit_bytes=limit * 1024 * 1024),
        cost_estimate=pl.CostEstimate(flops=cycles, bytes_accessed=0, transcendentals=0)
        if cycles
        else None,
        name=name,
    )(*args)


def swap(axis, first, block):
    pairs = [(i, i + 1) for i in range(first, lax.axis_size(axis) - 1, 2)]
    return lax.ppermute(block, axis, pairs + [(j, i) for i, j in pairs])


def everyone(block, axis):
    count = lax.axis_size(axis)
    copies = jnp.broadcast_to(block[None], (count,) + block.shape)
    return lax.all_to_all(copies, axis, split_axis=0, concat_axis=0, tiled=True)


def per_device(counts, classes, diffusivity, cotangent):
    shape = cotangent.shape
    counts, cotangent = (a.reshape(2, 8, 2, 16, 256) for a in (counts, cotangent))
    classes = classes.reshape(8, 2, 16, 256)
    (start,) = call(first_kernel, [(8, 128)], [], (), "first", 8, cycles=10**9)
    (table,) = call(table_kernel, [(16, 128)], [], (diffusivity,), "table", 8)
    own, across, inside = call(
        turn_kernel,
        [(16, 3, 16, 256), (8, 3, 16, 128), (8, 3, 16, 128)], [],
        (cotangent, classes, start), "turn", 8,
    )
    across, inside = swap("gy", 1, across), swap("gy", 0, inside)
    strip = (3 * HX - 2, 16, 256)
    mfirst, msecond = call(cut_strips, [strip, strip], [], (own,), "strips", 8)
    mfirst, msecond = swap("gx", 1, mfirst), swap("gx", 0, msecond)
    strip = (3 * HX - 2, 16, 128)
    edge, sfirst, ssecond = call(
        edge_kernel, [(16, 3, 16, 128), strip, strip], [], (across, inside), "edge", 8
    )
    sfirst, ssecond = swap("gx", 1, sfirst), swap("gx", 0, ssecond)
    level0, level1 = (2, NPL, 16, LN), (2, N1, 8, LN)
    fine = [level0] * 6 + [level1] * 6 + [level0] * 2 + [level1]
    kept = call(own_kernel, fine, [], (table, own, edge, mfirst, msecond), "own", 8, cycles=10**7)
    strip = (9, 8, LN)
    first, second, *kept = call(
        near_kernel,
        [strip, strip] + fine, [],
        (table, sfirst, ssecond, *kept), "near", 8,
        aliases={3 + n: 2 + n for n in range(15)},
    )
    keep0, keep1, d1 = kept[:6], kept[6:12], kept[14]
    first, second = swap("gx", 1, first), swap("gx", 0, second)
    zs = (4, 16, 128)
    *keep1, v1, react, diff2, matrix = call(
        inner_kernel, [level1] * 7 + [(16, 2, 16, 256), (3, 8, 128), (LN, 128)], [zs],
        (d1, counts, *keep1), "inner", 8,
        aliases={2 + n: n for n in range(6)}, cycles=10**7, dtypes=[F32] * 9 + [BF16],
    )
    message, *keep1, _, _ = call(
        outer_kernel, [(2, 3, 8, 128)] + [level1] * 8, [zs],
        (first, second, diff2, matrix, *keep1, v1, d1), "outer", 8,
        aliases={4 + n: 1 + n for n in range(8)},
    )
    gathered = everyone(message, "gx")
    tile, keep2, keep3 = call(
        middle_kernel,
        [(8, 128), (6, X2 + 2 * PAD, 8, 128), (6, X3 + 2 * PAD, 8, 128)],
        [(X2 + 2 * PAD, 8, 128), (X3 + 2 * PAD, 8, 128)] * 2 + [(2, 128, 128)],
        (gathered,), "middle", 8,
    )
    tiles = everyone(tile, "gy")
    (gradient,) = call(
        up_kernel,
        [(2, 8, 2, 16, 256)],
        [
            (2, X4 + 16, 128), (128, 128), (10, 8, 128), (12, 8, 128),
            (2, N1, 8, LN), (2, N1, 8, LN), (2, NPL, 16, LN),
        ],
        (tiles, keep2, keep3, react, *keep0, *keep1), "up", 12,
    )
    return gradient.reshape(shape)


def solution(mesh):
    in_specs = (P(None, None, "gx", "gy"), P(None, "gx", "gy"), P(), P(None, None, "gx", "gy"))
    out_specs = P(None, None, "gx", "gy")
    return jax.shard_map(
        per_device, mesh=mesh, in_specs=in_specs, out_specs=out_specs, check_vma=False
    )
```

```python
import jax
import jax.numpy as jnp
from jax import lax
from jax.experimental import pallas as pl
from jax.experimental.pallas import tpu as pltpu
from jax.sharding import PartitionSpec as P

F32 = jnp.float32
BF16 = jnp.bfloat16
RELAX = 0.8
REACT = 0.3
STEP = 256.0
COARSE_SWEEPS = 8

HX = 4
NPL = 16 + 2 * HX
N1 = 20
HY = 64
LN = 384
PAD = 4
X2 = 64
X3 = 32
X4 = 16


def iota(shape, axis):
    return lax.broadcasted_iota(jnp.int32, shape, axis)


def shift_up(value, by, axis):
    return pltpu.roll(value, by, axis)


def shift_down(value, by, axis):
    return pltpu.roll(value, value.shape[axis] - by, axis)


def reciprocal(x):
    return pl.reciprocal(x, approx=True)


def z_up(value, step):
    if step:
        return shift_up(value, step, 0)
    return jnp.concatenate([shift_up(value[8:], 1, 0), value[:8]], axis=0)


def z_down(value, step):
    if step:
        return shift_down(value, step, 0)
    return jnp.concatenate([value[8:], shift_down(value[:8], 1, 0)], axis=0)


def harm(a, b):
    return a * b * reciprocal(a + b)


def residual(u, b, fx, fxn, wy, wz, sy, sz):
    fy = wy * (u - shift_up(u, sy, 1))
    mu = u + (fx - fxn) + (fy - shift_down(fy, sy, 1))
    fz = wz * (u - z_up(u, sz))
    return b - (mu + (fz - z_down(fz, sz)))


def residual_short(u, b, fx, fxn, wy, wz, sy, sz):
    fy = wy * (u - shift_up(u, sy, 1)) - shift_down(wy, sy, 1) * (shift_down(u, sy, 1) - u)
    fz = wz * (u - z_up(u, sz)) - z_down(wz, sz) * (z_down(u, sz) - u)
    return b - (u + (fx - fxn) + (fy + fz))


def diagonal(wx, wxn, wy, wz, sy, sz):
    return 1.0 + (wx + wxn) + (wy + shift_down(wy, sy, 1)) + (wz + z_down(wz, sz))


def pair_lanes(value, half):
    width = value.shape[1]
    total = value + shift_down(value, half, 1)
    first = (iota(value.shape, 1) // half) % 2 == 0
    return jnp.where(first, total, shift_up(total, half, 1))


def pair_rows(value, half):
    total = value + shift_down(value, half, 0)
    first = (iota(value.shape, 0) // half) % 2 == 0
    return jnp.where(first, total, shift_up(total, half, 0))


def pick_lanes(value, lanes):
    return jnp.take_along_axis(value, jnp.broadcast_to(lanes, value.shape), axis=1)


def stencil(u, b, wx, wy, wz, start, count, sy, sz):
    here = u[start]
    fx = wx[start] * (here - u[start - 1])
    for j in range(count):
        p = start + j
        after = u[p + 1]
        fxn = wx[p + 1] * (after - here)
        yield p, here, residual(here, b[p], fx, fxn, wy[p], wz[p], sy, sz)
        here, fx = after, fxn


def pair_sums(residuals):
    sums, first = [], None
    for _, _, r in residuals:
        if first is None:
            first = r
        else:
            sums.append(first + r)
            first = None
    return sums


def face_weights(d, wx, wy, wz, inv, b, u, start, count, factor_x, my, mz, sy, sz):
    here = d[start]
    side = factor_x(start) * harm(here, d[start - 1])
    for j in range(count):
        p = start + j
        after = d[p + 1]
        siden = factor_x(p + 1) * harm(after, here)
        y = my * harm(here, shift_up(here, sy, 1))
        z = mz * harm(here, z_up(here, sz))
        wx[p], wy[p], wz[p] = side, y, z
        value = RELAX * reciprocal(diagonal(side, siden, y, z, sy, sz))
        inv[p] = value
        u[p] = value * b[p]
        here, side = after, siden


def blocks(lo, hi, size, body):
    assert (hi - lo) % size == 0
    if hi - lo == size:
        body(lo)
        return

    def step(n, carry):
        body(lo + n * size)
        return carry

    lax.fori_loop(0, (hi - lo) // size, step, 0)


def table_kernel(diff_ref, table):
    for s in range(2):
        for c in range(8):
            value = diff_ref[pl.ds(s, 1), pl.ds(c, 1)]
            table[pl.ds(8 * s + c, 1), :] = jnp.broadcast_to(value, (1, 128))


def first_kernel(out):
    out[...] = jnp.zeros((8, 128), F32)


def turn_kernel(cot, cls, start, own, across, inside):
    odd = lax.axis_index("gy") % 2 == 1
    left_half = iota((16, 128), 1) < HY
    for f in range(3):
        for k in range(8):
            pair = []
            for x in (k, k + 8):
                halves = [cls[:, n, x, :] if f == 2 else cot[f, :, n, x, :] for n in range(2)]
                pair.append(jnp.concatenate(halves, axis=0).astype(F32))
                own[x, f] = pair[-1]
            a, b = pair
            to_left = jnp.where(left_half, a[:, :128], pltpu.roll(b[:, :128], HY, 1))
            to_right = jnp.where(left_half, pltpu.roll(b[:, 128:], HY, 1), a[:, 128:])
            across[k, f] = jnp.where(odd, to_right, to_left)
            inside[k, f] = jnp.where(odd, to_left, to_right)


def cut_strips(planes, first, second):
    odd = lax.axis_index("gx") % 2 == 1
    for f in range(3):
        place = 0 if f == 2 else HX + f * (HX - 1)
        count = HX if f == 2 else HX - 1
        for n in range(count):
            low, high = planes[n, f], planes[16 - count + n, f]
            first[place + n] = jnp.where(odd, high, low)
            second[place + n] = jnp.where(odd, low, high)


def edge_kernel(across, inside, edge, first, second):
    odd = lax.axis_index("gy") % 2 == 1
    left_half = iota((16, 128), 1) < HY
    for k in range(8):
        for f in range(3):
            got = across[k, f], inside[k, f]
            fl, fr = jnp.where(odd, got[1], got[0]), jnp.where(odd, got[0], got[1])
            edge[k, f] = jnp.where(left_half, fr, fl)
            edge[k + 8, f] = pltpu.roll(jnp.where(left_half, fl, fr), HY, 1)
    cut_strips(edge, first, second)


def fine_tools(table, keep0, keep1, d0, v0, d1):
    gx = lax.axis_index("gx")
    gy = lax.axis_index("gy")
    nx = 16 * lax.axis_size("gx")
    ny = 256 * lax.axis_size("gy")
    b0, u0, b1 = keep0[0], keep0[5], keep1[0]

    def look_up(values):
        cls = values.astype(jnp.int32)
        bits = [(cls & (1 << n)) != 0 for n in range(3)]
        out = []
        for s in range(2):
            rows = [jnp.broadcast_to(table[pl.ds(8 * s + c, 1), :], (16, 128)) for c in range(8)]
            rows = [jnp.concatenate([r] * (cls.shape[1] // 128), axis=1) for r in rows]
            rows = [jnp.where(bits[0], rows[2 * n + 1], rows[2 * n]) for n in range(4)]
            rows = [jnp.where(bits[1], rows[2 * n + 1], rows[2 * n]) for n in range(2)]
            out.append(jnp.where(bits[2], rows[1], rows[0]))
        return out

    def assemble_own(own, edge, size):
        def body(start):
            for j in range(size):
                x = start + j
                planes = [jnp.concatenate([own[x, f], edge[x, f]], axis=1) for f in range(3)]
                for s, d in enumerate(look_up(planes[2])):
                    b0[s, x + HX] = planes[s]
                    d0[s, x + HX] = d

        blocks(0, 16, size, body)

    def assemble_strip(strips, high, cut):
        second = (gx + high) % 2 == 1

        def plane(n):
            return jnp.where(second, strips[1][n], strips[0][n])

        lo = 20 * high
        for j in range(HX):
            for s, d in enumerate(look_up(plane(j))):
                d0[s, lo + j, :, cut] = d
        for s in range(2):
            for n in range(HX - 1):
                b0[s, lo + 1 - high + n, :, cut] = plane(HX + s * (HX - 1) + n)

    def masks(rows, step, factor, origin):
        lane = iota((rows, LN), 1)
        ypos = gy * 256 + jnp.where(lane < 256 + HY, lane, lane - LN)
        my = jnp.where((ypos >= step) & (ypos < ny), F32(factor), F32(0.0))
        mz = jnp.where(iota((rows, LN), 0) >= 1, F32(factor), F32(0.0))

        def factor_x(p):
            xpos = (gx * 16) // step + p - origin
            return jnp.where((xpos >= 1) & (xpos < nx // step), F32(factor), F32(0.0))

        return my, mz, factor_x

    def weigh(lo, hi, size, rows, step, factor, d, keep, v):
        blocks(lo, hi, size, weigher(size, rows, step, factor, d, keep, v))

    def weigher(size, rows, step, factor, d, keep, v):
        my, mz, factor_x = masks(rows, step, factor, HX if step == 1 else 6)

        def body(start):
            for s in range(2):
                face_weights(
                    d.at[s], keep[1].at[s], keep[2].at[s], keep[3].at[s], keep[4].at[s],
                    keep[0].at[s], v.at[s], start, size, factor_x, my, mz, step, 0 if step == 1 else 1,
                )

        return body

    def planes(keep, u, s, start, size, step):
        return stencil(
            u.at[s], keep[0].at[s], keep[1].at[s], keep[2].at[s], keep[3].at[s],
            start, size, step, 0 if step == 1 else 1,
        )

    def smooth(lo, hi, size, keep, v, step):
        blocks(lo, hi, size, smoother(size, keep, v, step))

    def smoother(size, keep, v, step):
        def body(start):
            for s in range(2):
                for p, here, r in planes(keep, v, s, start, size, step):
                    keep[5][s, p] = here + keep[4][s, p] * r

        return body

    def restrict(lo, hi, size):
        blocks(lo, hi, size, restricter(size))

    def restricter(size):
        def body(start):
            for s in range(2):
                res = [r for _, _, r in planes(keep0, u0, s, 2 * start - 8, 2 * size, 1)]
                for i in range(size):
                    total = res[2 * i] + res[2 * i + 1]
                    b1[s, start + i] = 0.125 * pair_lanes(total[:8] + total[8:], 1)

        return body

    def coarse_diff(lo, hi, size):
        def body(start):
            for i in range(size):
                for s in range(2):
                    p = 2 * (start + i) - 8
                    total = d0[s, p] + d0[s, p + 1]
                    d1[s, start + i] = 0.125 * pair_lanes(total[:8] + total[8:], 1)

        blocks(lo, hi, size, body)

    at = assemble_strip, weigher, smoother, restricter
    return assemble_own, at, weigh, smooth, restrict, coarse_diff, planes


FINE = 2.0 * STEP
COARSER = 0.5 * STEP


def own_kernel(table, own, edge, mfirst, msecond, *refs):
    keep0, keep1, (d0, v0, d1) = refs[:6], refs[6:12], refs[12:]
    assemble_own, at, weigh, smooth, restrict, coarse_diff, _ = fine_tools(
        table, keep0, keep1, d0, v0, d1
    )

    def one_side(high, carry):
        at[0]((mfirst, msecond), high, slice(0, 256))
        return carry

    lax.fori_loop(0, 2, one_side, 0)
    assemble_own(own, edge, 4)
    weigh(5, 19, 7, 16, 1, FINE, d0, keep0, v0)
    smooth(6, 18, 4, keep0, v0, 1)
    restrict(8, 12, 2)
    coarse_diff(6, 14, 4)


def near_kernel(
    table, sfirst, ssecond, *refs,
):
    first, second, *refs = refs[15:]
    keep0, keep1, (d0, v0, d1) = refs[:6], refs[6:12], refs[12:]
    _, at, _, _, _, _, _ = fine_tools(table, keep0, keep1, d0, v0, d1)
    assemble_strip, weigher, smoother, restricter = at
    weigh = weigher(4, 16, 1, FINE, d0, keep0, v0)
    smooth = smoother(4, keep0, v0, 1)
    restrict = restricter(2)

    def one_side(high, carry):
        assemble_strip((sfirst, ssecond), high, slice(256, LN))
        weigh(1 + 18 * high)
        smooth(2 + 16 * high)
        restrict(6 + 6 * high)
        return carry

    lax.fori_loop(0, 2, one_side, 0)
    odd = lax.axis_index("gx") % 2 == 1
    even_lane = iota((8, LN), 1) % 2 == 0

    def send(n, ref, low, high):
        low, high = (jnp.where(even_lane, ref[0, m], ref[1, m]) for m in (low, high))
        first[n] = jnp.where(odd, high, low)
        second[n] = jnp.where(odd, low, high)

    for k in range(4):
        send(k, keep1[0], 6 + k, 10 + k)
    for k in range(5):
        send(4 + k, d1, 6 + k, 9 + k)


def averaging(shape, dtype):
    group = iota(shape, 0) // 4
    target = jnp.where(group < (256 + HY) // 4, group + 16, group - 80)
    return jnp.where(iota(shape, 1) == target, F32(0.0625), F32(0.0)).astype(dtype)


def to_level2(rows, matrix, zs, message):
    rows = jnp.concatenate(rows, axis=0)
    high = rows.astype(BF16)
    rest = rows - high.astype(F32)
    middle = rest.astype(BF16)
    low = (rest - middle.astype(F32)).astype(BF16)
    whole = jnp.dot(
        jnp.concatenate([high, middle, low], axis=0), matrix, preferred_element_type=F32
    )
    whole = whole[0:64] + whole[64:128] + whole[128:192]
    lane = iota((8, 128), 1)
    halved = []
    for n in range(4):
        part = zs.at[n]
        part[...] = whole[16 * n : 16 * (n + 1)]
        halved.append(part[pl.ds(0, 8, stride=2), :] + part[pl.ds(1, 8, stride=2), :])
    for k in range(3):
        message[k] = jnp.where(lane < 96, halved[k], pltpu.roll(halved[3], 96 - 32 * k, 1))


def inner_kernel(d1, counts, *refs):
    keep1, (v1, react, diff2, matrix, zs) = refs[6:12], refs[12:]
    _, _, weigh, smooth, _, _, _ = fine_tools(None, keep1, keep1, None, None, d1)
    weigh(7, 13, 6, 8, 2, COARSER, d1, keep1, v1)
    smooth(8, 12, 4, keep1, v1, 2)
    for s in range(2):
        for x in range(16):
            halves = [counts[s, :, n, x, :] for n in range(2)]
            react[x, s] = REACT * (0.25 * jnp.concatenate(halves, axis=0).astype(F32))
    matrix[...] = averaging((LN, 128), BF16)
    rows = [d1[s, 6 + 2 * n] + d1[s, 7 + 2 * n] for n in range(4) for s in range(2)]
    to_level2(rows, matrix[...], zs, diff2)


def outer_kernel(first, second, diff2, matrix, *refs):
    message, *refs = refs[8:]
    keep1, (v1, d1, zs) = refs[:6], refs[6:]
    _, _, weigh, smooth, _, _, planes = fine_tools(None, keep1, keep1, None, None, d1)
    gx = lax.axis_index("gx")
    last = lax.axis_size("gx") - 1
    odd = gx % 2 == 1
    even_lane = iota((8, LN), 1) % 2 == 0

    def both(got, ref, m, real=None):
        if real is not None:
            got = jnp.where(real, got, F32(1.0))
        ref[0, m] = jnp.where(even_lane, got, shift_up(got, 1, 1))
        ref[1, m] = jnp.where(even_lane, shift_down(got, 1, 1), got)

    for k in range(9):
        low = jnp.where(odd, second[k], first[k])
        high = jnp.where(odd, first[k], second[k])
        if k < 4:
            both(low, keep1[0], 2 + k)
            both(high, keep1[0], 14 + k)
        else:
            both(low, d1, k - 3, gx > 0)
            both(high, d1, 10 + k, gx < last)
    for start in (2, 13):
        weigh(start, start + 5, 5, 8, 2, COARSER, d1, keep1, v1)
    for start in (3, 12):
        smooth(start, start + 5, 5, keep1, v1, 2)
    res = [pair_sums(planes(keep1, keep1[5], s, 6, 8, 2)) for s in range(2)]
    rows = [res[s][n] for n in range(4) for s in range(2)]
    to_level2(rows, matrix[...], zs, message.at[0])
    message[1] = diff2[...]


def middle_kernel(gathered, tile, keep2, keep3, d2, d3, v2, v3, coarse):
    gy = lax.axis_index("gy")
    ny = 256 * lax.axis_size("gy")
    lane = iota((8, 128), 1)
    row = iota((8, 128), 0)
    ypos = gy * 64 + lane - 16
    zero = jnp.zeros((8, 128), F32)

    for keep, d, v, count in ((keep2, d2, v2, X2), (keep3, d3, v3, X3)):
        for k in range(PAD):
            for n in range(6):
                keep[n, k] = zero
                keep[n, count + PAD + k] = zero
        for p in (PAD - 1, PAD + count):
            d[p] = zero + 1.0
            v[p] = zero

    def level(keep, d, v, count, size, sy, sz, scale, nyl):
        factor = 2.0 * STEP * scale
        my = jnp.where((ypos >= sy) & (ypos < nyl), F32(factor), F32(0.0))
        mz = jnp.where(row % 4 >= sz, F32(factor), F32(0.0))

        def factor_x(p):
            return jnp.where((p > PAD) & (p < PAD + count), F32(factor), F32(0.0))

        def weights(start):
            face_weights(
                d, keep.at[1], keep.at[2], keep.at[3], keep.at[4], keep.at[0], v,
                start, size, factor_x, my, mz, sy, sz,
            )

        def planes(u, start, amount):
            return stencil(
                u, keep.at[0], keep.at[1], keep.at[2], keep.at[3], start, amount, sy, sz
            )

        def smooth(start):
            for p, here, r in planes(v, start, count):
                keep[5, p] = here + keep[4, p] * r

        blocks(PAD, PAD + count, size, weights)
        blocks(PAD, PAD + count, count, smooth)
        return planes

    for g in range(X2 // 4):
        for f, ref in ((0, keep2.at[0]), (1, d2)):
            packed = [gathered[g, f, k] for k in range(3)]
            fourth = [pltpu.roll(packed[k], 32 * (k + 1), 1) for k in range(3)]
            fourth = jnp.where(lane < 32, fourth[0], jnp.where(lane < 64, fourth[1], fourth[2]))
            for k, plane in enumerate(packed + [fourth]):
                ref[PAD + 4 * g + k] = plane
    planes2 = level(keep2, d2, v2, X2, X2, 1, 1, 0.0625, ny // 4)

    def restrict(start):
        first = 2 * (start - PAD) + PAD
        res = pair_sums(planes2(keep2.at[5], first, X2))
        for i in range(X3):
            total = res[i]
            keep3[0, start + i] = 0.125 * pair_rows(pair_lanes(total, 1), 1)
            total = d2[first + 2 * i] + d2[first + 2 * i + 1]
            d3[start + i] = 0.125 * pair_rows(pair_lanes(total, 1), 1)

    blocks(PAD, PAD + X3, X3, restrict)
    planes3 = level(keep3, d3, v3, X3, 32, 2, 2, 0.015625, ny // 4)

    def gather_pair(total):
        total = total + shift_down(total, 2, 1)
        return total + shift_down(total, 2, 0)

    res = pair_sums(planes3(keep3.at[5], PAD, X3))
    for i in range(X4):
        coarse[0, pl.ds(8 * i, 8), :] = gather_pair(res[i])
        coarse[1, pl.ds(8 * i, 8), :] = gather_pair(d3[PAD + 2 * i] + d3[PAD + 2 * i + 1])
    total = jnp.zeros((8, 128), F32)
    for g in range(8):
        f, s, half = g // 4, (g // 2) % 2, g % 2
        part = coarse[f, pl.ds(64 * half + 4 * s, 8, stride=8), :]
        part = pick_lanes(part, 16 + 4 * (lane % 16))
        total = jnp.where(lane // 16 == g, part, total)
    tile[...] = 0.125 * total


def coarsest(tiles):
    ngy = tiles.shape[0]
    width = 16 * ngy
    lane_group = iota((8, 128), 1) // 16
    fields = []
    for g in range(8):
        halves = []
        for h in range(width // 128):
            total = jnp.zeros((8, 128), F32)
            for q in range(8):
                piece = tiles[8 * h + q]
                shift = (16 * q - 16 * g) % 128
                if shift:
                    piece = pltpu.roll(piece, shift, 1)
                total = jnp.where(lane_group == q, piece, total)
            halves.append(total)
        fields.append(jnp.concatenate(halves, axis=1))
    whole = [jnp.concatenate([fields[2 * n], fields[2 * n + 1]], axis=0) for n in range(4)]
    shape = whole[0].shape
    factor = 2.0 * STEP * 0.25**4
    mx = jnp.where(iota(shape, 0) >= 1, F32(factor), F32(0.0))
    my = jnp.where(iota(shape, 1) >= 1, F32(factor), F32(0.0))
    out = []
    for s in range(2):
        b, d = whole[s], whole[2 + s]
        wx = mx * harm(d, shift_up(d, 1, 0))
        wy = my * harm(d, shift_up(d, 1, 1))
        inv = RELAX / (1.0 + (wx + shift_down(wx, 1, 0)) + (wy + shift_down(wy, 1, 1)))

        u = start = inv * b
        up_x, down_x = inv * wx, inv * shift_down(wx, 1, 0)
        up_y, down_y = inv * wy, inv * shift_down(wy, 1, 1)
        for _ in range(COARSE_SWEEPS - 1):
            along_x = up_x * shift_up(u, 1, 0) + down_x * shift_down(u, 1, 0)
            along_y = up_y * shift_up(u, 1, 1) + down_y * shift_down(u, 1, 1)
            u = ((1.0 - RELAX) * u + start) + (along_x + along_y)
        out.append(u + jnp.sum(b - u) / (shape[0] * shape[1]))
    return out


def up_kernel(
    tiles, keep2, keep3, react, *refs,
):
    keep0, keep1, (out, c4, rep2, u3, u2, p1, q1, q0) = refs[:6], refs[6:12], refs[12:]
    gx = lax.axis_index("gx")
    gy = lax.axis_index("gy")

    solved = jnp.concatenate(coarsest(tiles), axis=0)
    width = solved.shape[1]
    solved = pltpu.roll(solved, (width + 4 - 16 * gy) % width, 1)[:, :128]
    near = pick_lanes(solved, iota((1, 128), 1) // 4)
    for t in range(2):
        c4[t, pl.ds(0, 8), :] = jnp.zeros((8, 128), F32)
        c4[t, pl.ds(8, X4), :] = near[X4 * t : X4 * (t + 1)]
        c4[t, pl.ds(8 + X4, 8), :] = jnp.zeros((8, 128), F32)
    first_species = iota((8, 128), 0) < 4

    def coarse_plane(k):
        rows = [
            jnp.broadcast_to(c4[t, pl.ds(gx + 6 + k, 1), :], (8, 128)) for t in range(2)
        ]
        return jnp.where(first_species, rows[0], rows[1])

    def sweeps(keep, base, u, count, sy, sz):
        for turn in range(2):
            lo, hi = 1 + turn, count - 1 - turn
            here = u[lo]
            fx = keep[1, base + lo] * (here - u[lo - 1])
            for i in range(lo, hi):
                after = u[i + 1]
                fxn = keep[1, base + i + 1] * (after - here)
                r = residual_short(
                    here, keep[0, base + i], fx, fxn,
                    keep[2, base + i], keep[3, base + i], sy, sz,
                )
                u[i] = here + keep[4, base + i] * r
                here, fx = after, fxn

    base3 = gx * 2
    for i in range(0, 10, 2):
        plane = coarse_plane(i // 2)
        u3[i] = keep3[5, base3 + i] + plane
        u3[i + 1] = keep3[5, base3 + i + 1] + plane
    sweeps(keep3, base3, u3, 10, 2, 2)
    base2 = gx * 4
    for i in range(12):
        u2[i] = keep2[5, base2 + i] + u3[min(2 + i // 2, 9)]
    sweeps(keep2, base2, u2, 12, 1, 1)

    for i in range(8):
        for k in range(2):
            rep2[pl.ds(16 * i + k, 8, stride=2), :] = u2[2 + i]
    quarter = iota((1, 128), 1) // 4
    edge = jnp.where(quarter < 16, quarter + 80, quarter - 16)
    flat = [pick_lanes(rep2[...], lanes) for lanes in (quarter + 16, quarter + 48, edge)]
    c2 = jnp.concatenate(flat, axis=1).reshape(8, 2, 8, LN)

    def planes(keep, u, s, start, size, step):
        return stencil(
            u.at[s], keep[0].at[s], keep[1].at[s], keep[2].at[s], keep[3].at[s],
            start, size, step, 0 if step == 1 else 1,
        )

    def smooth(lo, hi, size, keep, u, new, step):
        def body(start):
            for s in range(2):
                for p, here, r in planes(keep, u, s, start, size, step):
                    new[s, p] = here + keep[4][s, p] * r

        blocks(lo, hi, size, body)

    for i in range(3, 17):
        for s in range(2):
            p1[s, i] = keep1[5][s, i] + c2[(i - 6) // 2 + 2, s]
    smooth(4, 16, 12, keep1, p1, q1, 2)
    smooth(5, 15, 10, keep1, q1, p1, 2)

    def corrected_sweep(n, carry):
        start = 3 + 6 * n
        for s in range(2):
            spread = [p1[s, 5 + 3 * n + j] for j in range(4)]
            spread = [jnp.concatenate([c, c], axis=0) for c in spread]

            def corrected(j):
                return keep0[5][s, start - 1 + j] + spread[j // 2]

            here = corrected(1)
            fx = keep0[1][s, start] * (here - corrected(0))
            for j in range(6):
                p = start + j
                after = corrected(j + 2)
                fxn = keep0[1][s, p + 1] * (after - here)
                r = residual(here, keep0[0][s, p], fx, fxn, keep0[2][s, p], keep0[3][s, p], 1, 0)
                q0[s, p] = here + keep0[4][s, p] * r
                here = after
                fx = fxn
        return carry

    lax.fori_loop(0, 3, corrected_sweep, 0)

    def last(start):
        for pair in zip(*(planes(keep0, q0, s, start, 4, 1) for s in range(2))):
            p = pair[0][0]
            a0, a1 = (
                (here + keep0[4][s, p] * r)[:, :256] for s, (_, here, r) in enumerate(pair)
            )
            x = p - HX
            total = a0 + a1
            for s, value in enumerate((a0 - react[x, 1] * total, a1 - react[x, 0] * total)):
                out[s, :, 0, x, :] = value[:8]
                out[s, :, 1, x, :] = value[8:]

    blocks(4, 20, 4, last)


def call(
    kernel, outs, scratch, args, name, limit, kinds=None, aliases=None, cycles=0, dtypes=None
):
    spaces = {"v": pltpu.VMEM, "s": pltpu.SMEM}
    specs = [pl.BlockSpec(memory_space=spaces[k]) for k in kinds or "v" * len(args)]
    return pl.pallas_call(
        kernel,
        out_shape=[jax.ShapeDtypeStruct(o, d) for o, d in zip(outs, dtypes or [F32] * len(outs))],
        in_specs=specs,
        out_specs=[pl.BlockSpec(memory_space=pltpu.VMEM)] * len(outs),
        scratch_shapes=[pltpu.VMEM(s, F32) if isinstance(s, tuple) else s for s in scratch],
        input_output_aliases=aliases or {},
        compiler_params=pltpu.CompilerParams(vmem_limit_bytes=limit * 1024 * 1024),
        cost_estimate=pl.CostEstimate(flops=cycles, bytes_accessed=0, transcendentals=0)
        if cycles
        else None,
        name=name,
    )(*args)


def swap(axis, first, block):
    pairs = [(i, i + 1) for i in range(first, lax.axis_size(axis) - 1, 2)]
    return lax.ppermute(block, axis, pairs + [(j, i) for i, j in pairs])


def everyone(block, axis):
    count = lax.axis_size(axis)
    copies = jnp.broadcast_to(block[None], (count,) + block.shape)
    return lax.all_to_all(copies, axis, split_axis=0, concat_axis=0, tiled=True)


def per_device(counts, classes, diffusivity, cotangent):
    shape = cotangent.shape
    counts, cotangent = (a.reshape(2, 8, 2, 16, 256) for a in (counts, cotangent))
    classes = classes.reshape(8, 2, 16, 256)
    (start,) = call(first_kernel, [(8, 128)], [], (), "first", 8, cycles=10**9)
    (table,) = call(table_kernel, [(16, 128)], [], (diffusivity,), "table", 8)
    own, across, inside = call(
        turn_kernel,
        [(16, 3, 16, 256), (8, 3, 16, 128), (8, 3, 16, 128)], [],
        (cotangent, classes, start), "turn", 8,
    )
    across, inside = swap("gy", 1, across), swap("gy", 0, inside)
    strip = (3 * HX - 2, 16, 256)
    mfirst, msecond = call(cut_strips, [strip, strip], [], (own,), "strips", 8)
    mfirst, msecond = swap("gx", 1, mfirst), swap("gx", 0, msecond)
    strip = (3 * HX - 2, 16, 128)
    edge, sfirst, ssecond = call(
        edge_kernel, [(16, 3, 16, 128), strip, strip], [], (across, inside), "edge", 8
    )
    sfirst, ssecond = swap("gx", 1, sfirst), swap("gx", 0, ssecond)
    level0, level1 = (2, NPL, 16, LN), (2, N1, 8, LN)
    fine = [level0] * 6 + [level1] * 6 + [level0] * 2 + [level1]
    kept = call(own_kernel, fine, [], (table, own, edge, mfirst, msecond), "own", 8, cycles=10**7)
    strip = (9, 8, LN)
    first, second, *kept = call(
        near_kernel,
        [strip, strip] + fine, [],
        (table, sfirst, ssecond, *kept), "near", 8,
        aliases={3 + n: 2 + n for n in range(15)},
    )
    keep0, keep1, d1 = kept[:6], kept[6:12], kept[14]
    first, second = swap("gx", 1, first), swap("gx", 0, second)
    zs = (4, 16, 128)
    *keep1, v1, react, diff2, matrix = call(
        inner_kernel, [level1] * 7 + [(16, 2, 16, 256), (3, 8, 128), (LN, 128)], [zs],
        (d1, counts, *keep1), "inner", 8,
        aliases={2 + n: n for n in range(6)}, cycles=10**7, dtypes=[F32] * 9 + [BF16],
    )
    message, *keep1, _, _ = call(
        outer_kernel, [(2, 3, 8, 128)] + [level1] * 8, [zs],
        (first, second, diff2, matrix, *keep1, v1, d1), "outer", 8,
        aliases={4 + n: 1 + n for n in range(8)},
    )
    gathered = everyone(message, "gx")
    tile, keep2, keep3 = call(
        middle_kernel,
        [(8, 128), (6, X2 + 2 * PAD, 8, 128), (6, X3 + 2 * PAD, 8, 128)],
        [(X2 + 2 * PAD, 8, 128), (X3 + 2 * PAD, 8, 128)] * 2 + [(2, 128, 128)],
        (gathered,), "middle", 8,
    )
    tiles = everyone(tile, "gy")
    (gradient,) = call(
        up_kernel,
        [(2, 8, 2, 16, 256)],
        [
            (2, X4 + 16, 128), (128, 128), (10, 8, 128), (12, 8, 128),
            (2, N1, 8, LN), (2, N1, 8, LN), (2, NPL, 16, LN),
        ],
        (tiles, keep2, keep3, react, *keep0, *keep1), "up", 12,
    )
    return gradient.reshape(shape)


def solution(mesh):
    in_specs = (P(None, None, "gx", "gy"), P(None, "gx", "gy"), P(), P(None, None, "gx", "gy"))
    out_specs = P(None, None, "gx", "gy")
    return jax.shard_map(
        per_device, mesh=mesh, in_specs=in_specs, out_specs=out_specs, check_vma=False
    )
```
